256 devices in a mesh: batch: 4 (over x_lo, core), query: 64 (over y, z, x_hi).
Axes of the slice: x: 4 (x_hi: 2, x_lo: 2; x = x_hi * 2 + x_lo), y: 4, z: 8, core: 2. Of those that a mesh axis runs over, the one named last changes fastest.
Arguments:
- points: bfloat16 [4, 16384, 1024], P('batch', 'query'), may hold values from -100 to 100
- order: int32 [4, 64, 256], P('batch', 'query'), may hold values from 0 to 255, each once within a row
- cotangent: bfloat16 [4, 16384, 1024], P('batch', 'query'), may hold values from -6 to 6
- kv_cross: bfloat16 [4, 512, 2048], P('batch', 'query'), may hold values from -6 to 6
- self_qkv: bfloat16 [4, 512, 3072], P('batch', 'query'), may hold values from -400 to 400
- kv_weight: bfloat16 [1024, 2048], replicated, may hold values from -0.1875 to 0.1875
- out_weight: bfloat16 [1024, 1024], replicated, may hold values from -0.1875 to 0.1875
Outputs:
- grad_points: bfloat16 [4, 16384, 1024], P('batch', 'query')
- grad_latent: bfloat16 [4, 512, 1024], P('batch', 'query')
- grad_qkv: bfloat16 [4, 512, 3072], P('batch', 'query')
- grad_out_proj: float32 [1024, 1024], P('query')
The draws below stay inside these ranges and needn't reach their ends.
Inputs may be any that keep to these rules, and one draw needn't show every extreme that they name: `order`: each row of 256 entries holds every number from 0 to 255 once.
All inputs are finite; a program needn't handle non-finite values.
Results may differ from the reference program's by a relative error of at most 0.015.
Values may be sent and summed in bfloat16 or wider, within the bound.
A program may use at most 128 MiB of HBM per device.

```python
import jax
import jax.numpy as jnp
from jax import lax

D = 1024
HEADS = 16
HEAD_SIZE = 64
M = 512
Q_DEV = 256
QBLOCKS = 64
QTOT = 16384
SHAPES = 4


def cross_keys(key):
    key = jax.random.fold_in(key, 98)
    return jnp.clip(jax.random.normal(key, (SHAPES, M, D), jnp.float32), -6.0, 6.0)


def self_keys(key):
    key = jax.random.fold_in(key, 99)
    return jnp.clip(jax.random.normal(key, (SHAPES, M, D), jnp.float32), -6.0, 6.0)


def draw_kv_cross(key, part):
    keys = cross_keys(key)
    key = jax.random.fold_in(key, 11)
    values = jnp.clip(jax.random.normal(key, (SHAPES, M, D), jnp.float32), -6.0, 6.0)
    return jnp.concatenate([keys, values], axis=-1).astype(jnp.bfloat16)


def draw_points(key, part):
    key = jax.random.fold_in(key, 12)
    base = jnp.clip(jax.random.normal(key, (SHAPES, QTOT, D), jnp.float32), -6.0, 6.0)
    return base.astype(jnp.bfloat16)


def draw_self_qkv(key, part):
    keys = self_keys(key)
    key = jax.random.fold_in(key, 13)
    queries = jnp.clip(jax.random.normal(key, (SHAPES, M, D), jnp.float32), -6.0, 6.0)
    values = jnp.clip(jax.random.normal(jax.random.fold_in(key, 1), (SHAPES, M, D), jnp.float32), -6.0, 6.0)
    return jnp.concatenate([queries, keys, values], axis=-1).astype(jnp.bfloat16)


def block_scale(stream_key, extent, cuts, low, top_value):
    def one(axis_at, blocks):
        draws = jax.random.uniform(jax.random.fold_in(jax.random.fold_in(stream_key, 6), axis_at), (blocks,), jnp.float32, low / len(cuts), top_value / len(cuts))
        return jnp.repeat(jnp.exp(draws), extent[axis_at] // blocks).reshape((-1,) + (1,) * (len(extent) - axis_at - 1))

    level = one(*cuts[0])
    for cut in cuts[1:]:
        level = level * one(*cut)
    return level


def gaussian(key, shape, deviation, most, split=(), held_as=jnp.bfloat16):
    drawn = deviation * jax.random.normal(key, shape, jnp.float32)
    if split:
        drawn = drawn * block_scale(key, shape, split, -0.22, 0.18)
    return jnp.clip(drawn, -most, most).astype(held_as)


def setup_inputs(seed: int = 0) -> dict:
    arg_keys = jax.random.split(jax.random.key(seed), 8)
    points = draw_points(jax.random.fold_in(arg_keys[7], 71), 0)
    order = jax.vmap(lambda own: jax.random.permutation(own, Q_DEV))(jax.random.split(arg_keys[1], SHAPES * QBLOCKS)).reshape((SHAPES, QBLOCKS, Q_DEV)).astype(jnp.int32)
    cotangent = gaussian(arg_keys[2], (SHAPES, QTOT, D), 1.0, 6.0, ((0, 4), (1, 64)))
    kv_cross = draw_kv_cross(jax.random.fold_in(arg_keys[7], 71), 0)
    self_qkv = draw_self_qkv(jax.random.fold_in(arg_keys[7], 71), 0)
    kv_weight = gaussian(arg_keys[5], (D, 2 * D), D ** -0.5, 0.1875)
    out_weight = gaussian(arg_keys[6], (D, D), D ** -0.5, 0.1875)
    return {"points": points, "order": order, "cotangent": cotangent, "kv_cross": kv_cross, "self_qkv": self_qkv, "kv_weight": kv_weight, "out_weight": out_weight}


def cross_block(qrows, grows, keys, values, scale):
    scores = jnp.dot(qrows, keys.T, preferred_element_type=jnp.float32) * scale
    probs = jax.nn.softmax(scores, axis=-1)
    dprob = jnp.dot(grows, values.T, preferred_element_type=jnp.float32)
    delta = jnp.sum(probs * dprob, axis=-1, keepdims=True)
    dscore = (probs * (dprob - delta) * scale).astype(jnp.bfloat16)
    grad_rows = jnp.dot(dscore, keys, preferred_element_type=jnp.float32).astype(jnp.bfloat16)
    dkey = jnp.dot(dscore.T, qrows, preferred_element_type=jnp.float32)
    dvalue = jnp.dot(probs.astype(jnp.bfloat16).T, grows, preferred_element_type=jnp.float32)
    return grad_rows, dkey, dvalue


def one_shape(points, order, cotangent, kv_cross, self_qkv, kv_weight, out_weight):
    scale = 1.0 / (D ** 0.5)
    keys = kv_cross[:, :D]
    values = kv_cross[:, D:]
    point_ids = jnp.arange(QBLOCKS, dtype=jnp.int32)[:, None] * Q_DEV + order.astype(jnp.int32)
    grad_rows_in = cotangent[point_ids.reshape(-1)].reshape(QBLOCKS, Q_DEV, D)
    query_rows = points.reshape(QBLOCKS, Q_DEV, D)

    def step(carry, items):
        qrows, grows = items
        grad_rows, dkey, dvalue = cross_block(qrows, grows, keys, values, scale)
        return (carry[0] + dkey, carry[1] + dvalue), grad_rows

    zero = jnp.zeros((M, D), jnp.float32)
    (dkey, dvalue), grad_points = lax.scan(step, (zero, zero), (query_rows, grad_rows_in))
    dkv = jnp.concatenate([dkey, dvalue], axis=1)
    grad_latent = jnp.dot(dkv, kv_weight.astype(jnp.float32).T, precision=lax.Precision.HIGHEST).astype(jnp.bfloat16)

    sscale = 1.0 / (HEAD_SIZE ** 0.5)
    qh = self_qkv[:, :D].reshape(M, HEADS, HEAD_SIZE).astype(jnp.float32)
    kh = self_qkv[:, D:2 * D].reshape(M, HEADS, HEAD_SIZE).astype(jnp.float32)
    vh = self_qkv[:, 2 * D:].reshape(M, HEADS, HEAD_SIZE).astype(jnp.float32)
    sprobs = jax.nn.softmax(jnp.einsum("ihd,jhd->hij", qh, kh) * sscale, axis=-1)
    sprobs_low = sprobs.astype(jnp.bfloat16).astype(jnp.float32)
    attended = jnp.einsum("hij,jhd->ihd", sprobs_low, vh).reshape(M, D).astype(jnp.bfloat16)
    proj_term = jnp.dot(attended.T, grad_latent, preferred_element_type=jnp.float32)
    dattended = jnp.dot(grad_latent, out_weight.T, preferred_element_type=jnp.float32).astype(jnp.bfloat16)
    dah = dattended.reshape(M, HEADS, HEAD_SIZE).astype(jnp.float32)
    sdprob = jnp.einsum("ihd,jhd->hij", dah, vh)
    sdelta = jnp.sum(sprobs * sdprob, axis=-1, keepdims=True)
    sdscore = (sprobs * (sdprob - sdelta) * sscale).astype(jnp.bfloat16).astype(jnp.float32)
    dq = jnp.einsum("hij,jhd->ihd", sdscore, kh).reshape(M, D)
    dk = jnp.einsum("hij,ihd->jhd", sdscore, qh).reshape(M, D)
    dv = jnp.einsum("hij,ihd->jhd", sprobs_low, dah).reshape(M, D)
    grad_qkv = jnp.concatenate([dq, dk, dv], axis=1).astype(jnp.bfloat16)
    return grad_points.reshape(QTOT, D), grad_latent, grad_qkv, proj_term


def reference(points, order, cotangent, kv_cross, self_qkv, kv_weight, out_weight):
    grads_points = []
    grads_latent = []
    grads_qkv = []
    proj_total = jnp.zeros((D, D), jnp.float32)
    for shape_index in range(SHAPES):
        outs = one_shape(points[shape_index], order[shape_index], cotangent[shape_index],
                         kv_cross[shape_index], self_qkv[shape_index], kv_weight, out_weight)
        grads_points.append(outs[0])
        grads_latent.append(outs[1])
        grads_qkv.append(outs[2])
        proj_total = proj_total + outs[3]
    return (jnp.stack(grads_points), jnp.stack(grads_latent), jnp.stack(grads_qkv), proj_total)
```

```python
import functools

import jax
import jax.numpy as jnp
from jax import lax
from jax.experimental import pallas as pl
from jax.experimental.pallas import tpu as pltpu
from jax.sharding import PartitionSpec as P

MESH = pl.DeviceIdType.MESH
BF = jnp.bfloat16
F32 = jnp.float32


def nt(a, b):
    return lax.dot_general(a, b, (((1,), (1,)), ((), ())), preferred_element_type=F32)


def nn(a, b):
    return lax.dot_general(a, b, (((1,), (0,)), ((), ())), preferred_element_type=F32)


def tn(a, b):
    return lax.dot_general(a, b, (((0,), (0,)), ((), ())), preferred_element_type=F32)


GROUPS = dict(
    kvrow=2, qy=3, qz=7, qx=2, swap_q=1, swap_g=1, kz0=7, ky1=3, kz1=7, ky0=3, sib0=4, sib1=8,
    pair=1, ry=3, rz=7, gz=7, gy=3, gsib=4, lat=1, proj=4, oz=3, oy=4, pts=1,
)
BASE = {}
COUNT = 0
for _name, _n in GROUPS.items():
    BASE[_name] = COUNT
    COUNT += _n


def kernel(
    points, order, cot, kv, sqkv, wkv, wo,
    gpts, glat, gqkv, gproj,
    gsend, qb, gb, kvs, kvr, kvf, sq, r1, r2, r3, wkvb, wob, qg, spt, sp16, att,
    psend, precv, pown, ysend, yrecv, zsend, zrecv, zacc, dzf, pjf, pjs, pjr,
    ob, or1, or2, gls, glr, gps,
    ss, rs, ls,
):
    b = lax.axis_index("batch")
    k = lax.axis_index("query")
    xlo = b // 2
    c = b % 2
    y = k // 16
    z = (k // 2) % 8
    xhi = k % 2
    swapped = c != xhi
    kept = c == xhi

    def dev(xlo_, c_, y_, z_, xhi_):
        return (xlo_ * 2 + c_, (y_ * 8 + z_) * 2 + xhi_)

    sib = dev(xlo, 1 - c, y, z, xhi)
    diag = dev(xlo, xhi, y, z, c)
    heads4 = z // 2

    def dev_y(j):
        return dev(xlo, c, (y + j) % 4, z, xhi)

    def dev_z(j):
        return dev(xlo, c, y, (z + j) % 8, xhi)

    def rc(src, dst, i, to):
        return pltpu.make_async_remote_copy(
            src_ref=src, dst_ref=dst, send_sem=ss.at[i], recv_sem=rs.at[i],
            device_id=to, device_id_type=MESH,
        )

    def at(name, j=0):
        return BASE[name] + j

    barrier = pltpu.get_barrier_semaphore()
    greet = [sib, dev(xlo, 1 - c, y, z, 1 - xhi), dev(xlo, c, y, z, 1 - xhi)]
    greet += [dev_y(j) for j in (1, 2, 3)] + [dev_z(j) for j in range(1, 8)]
    greet += [dev(xlo, 1 - c, (y + j) % 4, z, 1 - xhi) for j in (1, 2, 3)]
    greet += [dev(1 - xlo, cc, y, z, xx) for cc in (0, 1) for xx in (0, 1)]
    for to in greet:
        pl.semaphore_signal(barrier, inc=1, device_id=to, device_id_type=MESH)

    head = y * 4 + heads4
    load_w = pltpu.make_async_copy(wkv, wkvb, ls.at[0])
    load_w.start()
    load_o = pltpu.make_async_copy(wo.at[pl.ds(pl.multiple_of(head * 64, 64), 64)], wob, ls.at[1])
    load_o.start()

    kvw = kv[0].astype(F32)
    for t in (0, 1):
        kvs[t] = jnp.concatenate(
            [kvw[:, t * 1024:t * 1024 + 512], kvw[:, t * 1024 + 512:t * 1024 + 1024]], axis=0
        ).astype(BF)
    sw = sqkv[0].astype(F32)
    pad = jnp.zeros((8, 64), F32)
    for h in range(16):
        top = jnp.concatenate([sw[:, h * 64:h * 64 + 64], sw[:, 1024 + h * 64:1024 + h * 64 + 64]], axis=1)
        low = jnp.concatenate([sw[:, 2048 + h * 64:2048 + h * 64 + 64], pad], axis=1)
        sq[h] = jnp.concatenate([top, low], axis=0).astype(BF)
    hot = (lax.broadcasted_iota(jnp.int32, (256, 256), 0) == order[0]).astype(F32).astype(BF)
    gsend[...] = tn(hot, cot[0]).astype(BF)

    pl.semaphore_wait(barrier, len(greet))

    def kvrow(t):
        return rc(kvs.at[t], kvr.at[xhi], at("kvrow") + xhi, dev(xlo, t, y, z, c))

    def kvrow_send(t):
        return pltpu.make_async_remote_copy(
            src_ref=kvs.at[t], dst_ref=kvr.at[xhi], send_sem=ss.at[at("kvrow", t)],
            recv_sem=rs.at[at("kvrow") + xhi], device_id=dev(xlo, t, y, z, c), device_id_type=MESH,
        )

    local_row = pltpu.make_async_copy(kvs.at[c], kvr.at[xhi], ls.at[2])
    for t in (0, 1):
        mine = jnp.logical_and(kept, c == t)

        @pl.when(jnp.logical_not(mine))
        def _():
            kvrow_send(t).start()

    @pl.when(kept)
    def _():
        local_row.start()

    for j in (1, 2, 3):
        yj = (y + j) % 4
        rc(sq.at[pl.ds(yj * 4, 4)], r1.at[y], at("qy", j - 1), dev_y(j)).start()
    local_qy = pltpu.make_async_copy(sq.at[pl.ds(y * 4, 4)], r1.at[y], ls.at[3])
    local_qy.start()

    swap_q = rc(points.at[0], qb, at("swap_q"), diag)
    local_q = pltpu.make_async_copy(points.at[0], qb, ls.at[4])
    swap_g = rc(gsend, gb, at("swap_g"), diag)
    local_g = pltpu.make_async_copy(gsend, gb, ls.at[5])

    @pl.when(swapped)
    def _():
        swap_q.start()
        swap_g.start()

    @pl.when(kept)
    def _():
        local_q.start()
        local_g.start()

    for blk in (0, 1):
        mine = jnp.logical_and(kept, xhi == blk)

        @pl.when(jnp.logical_not(mine))
        def _():
            rc(kvs.at[0], kvr.at[blk], at("kvrow", blk), sib).wait_recv()

    @pl.when(kept)
    def _():
        local_row.wait()

    p0 = kvr[0].astype(F32)
    p1 = kvr[1].astype(F32)
    kvf[c, 0, y, z] = jnp.concatenate([p0[:8], p1[:8]], axis=0).astype(BF)
    kvf[c, 1, y, z] = jnp.concatenate([p0[8:], p1[8:]], axis=0).astype(BF)

    def kz0(j, slot):
        return rc(kvf.at[c, 0, y, slot], kvf.at[c, 0, y, slot], at("kz0", j - 1), dev_z(j))

    def ky1(j, slot):
        return rc(kvf.at[c, 1, slot, z], kvf.at[c, 1, slot, z], at("ky1", j - 1), dev_y(j))

    def kz1(j, slot):
        return rc(kvf.at[c, 1, :, slot], kvf.at[c, 1, :, slot], at("kz1", j - 1), dev_z(j))

    def ky0(j, slot):
        return rc(kvf.at[c, 0, slot], kvf.at[c, 0, slot], at("ky0", j - 1), dev_y(j))

    def sib0(which, j, slot):
        return rc(kvf.at[which, 0, slot], kvf.at[which, 0, slot], at("sib0", j), sib)

    def sib1(which, j, slot):
        return rc(kvf.at[which, 1, :, slot], kvf.at[which, 1, :, slot], at("sib1", j), sib)

    for j in (1, 2, 3):
        ky1(j, y).start()
    for j in range(1, 8):
        kz0(j, z).start()

    for j in (1, 2, 3):
        rc(r1.at[0], r1.at[(y + 4 - j) % 4], at("qy", j - 1), sib).wait_recv()
    local_qy.wait()
    for j in range(1, 8):
        zj = (z + j) % 8
        rc(r1.at[:, zj // 2], r2.at[:, z], at("qz", j - 1), dev_z(j)).start()
    local_qz = pltpu.make_async_copy(r1.at[:, heads4], r2.at[:, z], ls.at[6])
    local_qz.start()

    for j in (1, 2, 3):
        ky1(j, (y + 4 - j) % 4).wait_recv()
    for j in range(1, 8):
        kz1(j, z).start()
    sib1(c, 0, z).start()

    for j in range(1, 8):
        rc(r1.at[:, 0], r2.at[:, (z + 8 - j) % 8], at("qz", j - 1), sib).wait_recv()
    local_qz.wait()

    def qx_send(t):
        return pltpu.make_async_remote_copy(
            src_ref=r2, dst_ref=r3.at[:, :, xhi], send_sem=ss.at[at("qx", t)],
            recv_sem=rs.at[at("qx") + xhi], device_id=dev(xlo, t, y, z, c), device_id_type=MESH,
        )

    local_qx = pltpu.make_async_copy(r2, r3.at[:, :, xhi], ls.at[7])
    for t in (0, 1):
        mine = jnp.logical_and(kept, c == t)

        @pl.when(jnp.logical_not(mine))
        def _():
            qx_send(t).start()

    @pl.when(kept)
    def _():
        local_qx.start()

    for j in range(1, 8):
        kz0(j, (z + 8 - j) % 8).wait_recv()
    for j in (1, 2, 3):
        ky0(j, y).start()
    sib0(c, 0, y).start()

    load_w.wait()

    @pl.when(swapped)
    def _():
        swap_q.wait_recv()

    @pl.when(kept)
    def _():
        local_q.wait()

    qw = nt(qb[...], wkvb[:, 0:1024]).astype(BF)
    qg[0, 0:256] = qw[:, 0:512]
    qg[1, 0:256] = qw[:, 512:1024]

    for blk in (0, 1):
        mine = jnp.logical_and(kept, xhi == blk)

        @pl.when(jnp.logical_not(mine))
        def _():
            rc(r2, r3.at[:, :, blk], at("qx", blk), sib).wait_recv()

    @pl.when(kept)
    def _():
        local_qx.wait()

    tiles = r3[...].astype(F32).reshape(64, 16, 128)
    top = tiles[:, :8].reshape(512, 128)
    low = tiles[:, 8:].reshape(512, 128)
    sq_q = top[:, :64].astype(BF)
    sq_k = top[:, 64:].astype(BF)
    sq_v = low[:, :64].astype(BF)
    sscale = 1.0 / 64 ** 0.5
    scores = nt(sq_k, sq_q) * sscale
    weights = jnp.exp(scores - jnp.max(scores, axis=0, keepdims=True))
    sprobs = weights / jnp.sum(weights, axis=0, keepdims=True)
    spt[...] = sprobs
    sp16[...] = sprobs.astype(BF)
    vt = low[:, :64].T.astype(BF)
    att[...] = nn(vt, sp16[...]).astype(BF)

    for j in range(1, 8):
        kz1(j, (z + 8 - j) % 8).wait_recv()
        sib1(c, j, (z + 8 - j) % 8).start()
    for j in (1, 2, 3):
        ky0(j, (y + 4 - j) % 4).wait_recv()
        sib0(c, j, (y + 4 - j) % 4).start()

    @pl.when(swapped)
    def _():
        swap_g.wait_recv()

    @pl.when(kept)
    def _():
        local_g.wait()

    gw = nt(gb[...], wkvb[:, 1024:2048]).astype(BF)
    qg[0, 256:512] = gw[:, 0:512]
    qg[1, 256:512] = gw[:, 512:1024]

    for j in range(8):
        sib1(1 - c, j, (z + 8 - j) % 8).wait_recv()
    for j in range(4):
        sib0(1 - c, j, (y + 4 - j) % 4).wait_recv()

    def half(t, h):
        return kvf[t, h].reshape(512, 512)

    scale = 1.0 / 1024 ** 0.5
    s = (nt(half(0, 0), qb[:, 0:512]) + nt(half(0, 1), qb[:, 512:1024])) * scale
    e = jnp.exp(s - jnp.max(s, axis=0, keepdims=True))
    p = e / jnp.sum(e, axis=0, keepdims=True)
    dp = nt(half(1, 0), gb[:, 0:512]) + nt(half(1, 1), gb[:, 512:1024])
    delta = jnp.sum(p * dp, axis=0, keepdims=True)
    ds = (p * (dp - delta) * scale).astype(BF)
    both = jnp.concatenate([ds, p.astype(BF)], axis=1)

    psend[...] = nn(both, qg[1 - c]).astype(BF).reshape(4, 128, 512)
    pair = rc(psend, precv, at("pair"), sib)
    pair.start()
    pown[...] = nn(both, qg[c]).reshape(4, 128, 512)
    gps[:, 0:512] = tn(ds, half(0, 0)).astype(BF)
    gps[:, 512:1024] = tn(ds, half(0, 1)).astype(BF)
    pts = rc(gps, gpts.at[0], at("pts"), diag)
    local_pts = pltpu.make_async_copy(gps, gpts.at[0], ls.at[8])
    pair.wait_recv()

    @pl.when(swapped)
    def _():
        pts.start()

    @pl.when(kept)
    def _():
        local_pts.start()

    for j in (1, 2, 3):
        yj = (y + j) % 4
        ysend[j - 1] = (pown[yj] + precv[yj].astype(F32)).astype(BF)
        rc(ysend.at[j - 1], yrecv.at[j - 1], at("ry", j - 1), dev_y(j)).start()
    acc = pown[y] + precv[y].astype(F32)
    for j in (1, 2, 3):
        rc(ysend.at[j - 1], yrecv.at[j - 1], at("ry", j - 1), dev_y(j)).wait_recv()
        acc = acc + yrecv[j - 1].astype(F32)
    zacc[...] = acc.reshape(8, 16, 512)
    zsend[...] = acc.astype(BF).reshape(8, 16, 512)
    for j in range(1, 8):
        rc(zsend.at[(z + j) % 8], zrecv.at[j - 1], at("rz", j - 1), dev_z(j)).start()
    acc = zacc[z]
    for j in range(1, 8):
        rc(zsend.at[j], zrecv.at[j - 1], at("rz", j - 1), dev_z(j)).wait_recv()
        acc = acc + zrecv[j - 1].astype(F32)
    dzf[c, y, z] = acc.astype(BF)

    def gz(j, slot):
        return rc(dzf.at[c, y, slot], dzf.at[c, y, slot], at("gz", j - 1), dev_z(j))

    def gy(j, slot):
        return rc(dzf.at[c, slot], dzf.at[c, slot], at("gy", j - 1), dev_y(j))

    def gsib(which, j, slot):
        return rc(dzf.at[which, slot], dzf.at[which, slot], at("gsib", j), sib)

    for j in range(1, 8):
        gz(j, z).start()
    for j in range(1, 8):
        gz(j, (z + 8 - j) % 8).wait_recv()
    for j in (1, 2, 3):
        gy(j, y).start()
    gsib(c, 0, y).start()
    for j in (1, 2, 3):
        gy(j, (y + 4 - j) % 4).wait_recv()
        gsib(c, j, (y + 4 - j) % 4).start()
    for j in range(4):
        gsib(1 - c, j, (y + 4 - j) % 4).wait_recv()

    load_o.wait()
    dz0 = dzf[0].reshape(512, 512)
    dz1 = dzf[1].reshape(512, 512)
    datt = (nt(dz0, wob[:, 0:512]) + nt(dz1, wob[:, 512:1024])).astype(BF)
    pjf[:, 0:512] = nn(att[...], dz0)
    pjf[:, 512:1024] = nn(att[...], dz1)
    pjs[...] = pjf[pl.ds(pl.multiple_of(((z % 2) * 2 + c) * 16, 16), 16), :].astype(BF)

    shape_at = xlo * 2 + xhi

    def proj_send(a, t):
        return pltpu.make_async_remote_copy(
            src_ref=pjs, dst_ref=pjr.at[shape_at], send_sem=ss.at[at("proj", a * 2 + t)],
            recv_sem=rs.at[at("proj") + shape_at], device_id=dev(a, t, y, z, c), device_id_type=MESH,
        )

    local_proj = pltpu.make_async_copy(pjs, pjr.at[shape_at], ls.at[9])

    def proj_mine(a, t):
        return jnp.logical_and(kept, jnp.logical_and(xlo == a, c == t))

    for a in (0, 1):
        for t in (0, 1):

            @pl.when(jnp.logical_not(proj_mine(a, t)))
            def _():
                proj_send(a, t).start()

    own0 = dzf[0, y, z].astype(F32)
    own1 = dzf[1, y, z].astype(F32)
    first = c == 0
    gls[...] = jnp.concatenate(
        [jnp.where(first, own0[:8], own0[8:]), jnp.where(first, own1[:8], own1[8:])], axis=0
    ).astype(BF)
    lat = rc(gls, glr, at("lat"), diag)
    local_lat = pltpu.make_async_copy(gls, glr, ls.at[10])

    @pl.when(swapped)
    def _():
        lat.start()

    @pl.when(kept)
    def _():
        local_proj.start()
        local_lat.start()

    sdp = nt(sq_v, datt)
    sprobs = spt[...]
    sdelta = jnp.sum(sprobs * sdp, axis=0, keepdims=True)
    sds = (sprobs * (sdp - sdelta) * sscale).astype(BF)
    dk = nn(sds, sq_q)
    dv = nn(sp16[...], datt)
    kt = top[:, 64:].T.astype(BF)
    dq = nn(kt, sds).T
    m1 = jnp.concatenate([dq, dk], axis=1).reshape(64, 8, 128)
    m2 = jnp.concatenate([dv, jnp.zeros((512, 64), F32)], axis=1).reshape(64, 8, 128)
    ob[...] = jnp.concatenate([m1, m2], axis=1).astype(BF).reshape(4, 8, 2, 16, 128)

    for j in (1, 2, 3):
        zj = (z + 2 * j) % 8
        rc(ob.at[:, zj, c], or1.at[heads4], at("oz", j - 1), dev_z(2 * j)).start()
    local_oz = pltpu.make_async_copy(ob.at[:, z, c], or1.at[heads4], ls.at[11])
    local_oz.start()
    for j in (1, 2, 3):
        rc(ob.at[:, 0, 0], or1.at[(heads4 + 4 - j) % 4], at("oz", j - 1), sib).wait_recv()
    local_oz.wait()

    def oy(j):
        yj = (y + j) % 4
        return rc(or1.at[:, yj], or2.at[y], at("oy", j), dev(xlo, xhi, yj, z, c))

    for j in (1, 2, 3):
        oy(j).start()
    local_oy = pltpu.make_async_copy(or1.at[:, y], or2.at[y], ls.at[12])

    @pl.when(swapped)
    def _():
        oy(0).start()

    @pl.when(kept)
    def _():
        local_oy.start()

    for src in range(4):

        @pl.when(jnp.logical_not(jnp.logical_and(kept, shape_at == src)))
        def _():
            rc(pjs, pjr.at[src], at("proj", src), sib).wait_recv()

    @pl.when(kept)
    def _():
        local_proj.wait()
        local_lat.wait()
        local_pts.wait()

    @pl.when(swapped)
    def _():
        lat.wait_recv()
        pts.wait_recv()

    total = pjr[0].astype(F32)
    for src in (1, 2, 3):
        total = total + pjr[src].astype(F32)
    gproj[...] = total
    lr = glr[...].astype(F32)
    glat[0] = jnp.concatenate([lr[:8], lr[8:]], axis=1).astype(BF)

    for j in (1, 2, 3):
        rc(or1.at[:, 0], or2.at[(y + 4 - j) % 4], at("oy", j), sib).wait_recv()

    @pl.when(swapped)
    def _():
        oy(0).wait_recv()

    @pl.when(kept)
    def _():
        local_oy.wait()

    res = or2[...].astype(F32).reshape(16, 16, 128)
    parts = [res[h, :8, 0:64] for h in range(16)]
    parts += [res[h, :8, 64:128] for h in range(16)]
    parts += [res[h, 8:, 0:64] for h in range(16)]
    gqkv[0] = jnp.concatenate(parts, axis=1).astype(BF)

    for t in (0, 1):
        mine = jnp.logical_and(kept, c == t)

        @pl.when(jnp.logical_not(mine))
        def _():
            kvrow_send(t).wait_send()
            qx_send(t).wait_send()

    for j in (1, 2, 3):
        rc(sq.at[pl.ds(0, 4)], r1.at[y], at("qy", j - 1), sib).wait_send()
        ky1(j, y).wait_send()
        ky0(j, y).wait_send()
        rc(ysend.at[j - 1], yrecv.at[j - 1], at("ry", j - 1), sib).wait_send()
        gy(j, y).wait_send()
        rc(ob.at[:, 0, 0], or1.at[0], at("oz", j - 1), sib).wait_send()
        oy(j).wait_send()
    for j in range(1, 8):
        kz0(j, z).wait_send()
        kz1(j, z).wait_send()
        rc(r1.at[:, 0], r2.at[:, z], at("qz", j - 1), sib).wait_send()
        rc(zsend.at[j], zrecv.at[j - 1], at("rz", j - 1), sib).wait_send()
        gz(j, z).wait_send()
    for j in range(8):
        sib1(c, j, (z + 8 - j) % 8).wait_send()
    for j in range(4):
        sib0(c, j, (y + 4 - j) % 4).wait_send()
        gsib(c, j, (y + 4 - j) % 4).wait_send()
    pair.wait_send()
    for a in (0, 1):
        for t in (0, 1):

            @pl.when(jnp.logical_not(proj_mine(a, t)))
            def _():
                proj_send(a, t).wait_send()

    @pl.when(swapped)
    def _():
        swap_q.wait_send()
        swap_g.wait_send()
        pts.wait_send()
        lat.wait_send()
        oy(0).wait_send()


def on_device(points, order, cotangent, kv_cross, self_qkv, kv_weight, out_weight):
    vmem = pl.BlockSpec(memory_space=pltpu.VMEM)
    hbm = pl.BlockSpec(memory_space=pl.ANY)
    scratch = [
        ((256, 1024), BF),
        ((256, 1024), BF),
        ((256, 1024), BF),
        ((2, 16, 512), BF),
        ((2, 16, 512), BF),
        ((2, 2, 4, 8, 16, 512), BF),
        ((16, 16, 128), BF),
        ((4, 4, 16, 128), BF),
        ((4, 8, 16, 128), BF),
        ((4, 8, 2, 16, 128), BF),
        ((1024, 2048), BF),
        ((64, 1024), BF),
        ((2, 512, 512), BF),
        ((512, 512), F32),
        ((512, 512), BF),
        ((64, 512), BF),
        ((4, 128, 512), BF),
        ((4, 128, 512), BF),
        ((4, 128, 512), F32),
        ((3, 128, 512), BF),
        ((3, 128, 512), BF),
        ((8, 16, 512), BF),
        ((7, 16, 512), BF),
        ((8, 16, 512), F32),
        ((2, 4, 8, 16, 512), BF),
        ((64, 1024), F32),
        ((16, 1024), BF),
        ((4, 16, 1024), BF),
        ((4, 8, 2, 16, 128), BF),
        ((4, 4, 16, 128), BF),
        ((4, 4, 16, 128), BF),
        ((16, 512), BF),
        ((16, 512), BF),
        ((256, 1024), BF),
    ]
    return pl.pallas_call(
        kernel,
        out_shape=(
            jax.ShapeDtypeStruct((1, 256, 1024), BF),
            jax.ShapeDtypeStruct((1, 8, 1024), BF),
            jax.ShapeDtypeStruct((1, 8, 3072), BF),
            jax.ShapeDtypeStruct((16, 1024), F32),
        ),
        in_specs=[hbm, vmem, vmem, vmem, vmem, hbm, hbm],
        out_specs=(vmem, vmem, vmem, vmem),
        scratch_shapes=[pltpu.VMEM(shape, dtype) for shape, dtype in scratch]
        + [pltpu.SemaphoreType.DMA((COUNT,)), pltpu.SemaphoreType.DMA((COUNT,)), pltpu.SemaphoreType.DMA((13,))],
        name="fused_backward",
        cost_estimate=pl.CostEstimate(flops=3_000_000_000, bytes_accessed=8_000_000, transcendentals=400_000),
        compiler_params=pltpu.CompilerParams(
            collective_id=0, has_side_effects=True, vmem_limit_bytes=56 * 1024 * 1024
        ),
    )(points, order, cotangent, kv_cross, self_qkv, kv_weight, out_weight)


def solution(mesh):
    rows = P("batch", "query", None)
    return jax.shard_map(
        on_device,
        mesh=mesh,
        in_specs=(rows, rows, rows, rows, rows, P(), P()),
        out_specs=(rows, rows, rows, P("query", None)),
        check_vma=False,
    )
```

```python
import functools

import jax
import jax.numpy as jnp
from jax import lax
from jax.experimental import pallas as pl
from jax.experimental.pallas import tpu as pltpu
from jax.sharding import PartitionSpec as P

MESH = pl.DeviceIdType.MESH
BF = jnp.bfloat16
F32 = jnp.float32


def nt(a, b):
    return lax.dot_general(a, b, (((1,), (1,)), ((), ())), preferred_element_type=F32)


def nn(a, b):
    return lax.dot_general(a, b, (((1,), (0,)), ((), ())), preferred_element_type=F32)


def tn(a, b):
    return lax.dot_general(a, b, (((0,), (0,)), ((), ())), preferred_element_type=F32)


GROUPS = dict(
    kvrow=2, qy=3, qz=7, qx=2, swap_q=1, swap_g=1, kz=7, ky=24, ks=4,
    pair=4, ry=24, rz=7, gz=7, gy=24, gs=4, lat=1, proj=4, back=16, pts=1,
)
MIX_Z = (4, 1, 7, 2, 6, 3, 5)
FAR_Z = (4, 3, 5, 2, 6, 1, 7)
NEAR_Z = (1, 7, 2, 6, 3, 5, 4)
ARRIVE_Z = (1, 7, 2, 6, 4, 3, 5)
FAR_Y = (2, 1, 3)
NEAR_ROWS = (0, 1, 7, 2)
BASE = {}
COUNT = 0
for _name, _n in GROUPS.items():
    BASE[_name] = COUNT
    COUNT += _n


def kernel(
    points, order, cot, kv, sqkv, wkv, wo,
    gpts, or2, glr, pjr,
    cotb, gsend, qb, gb, kvs, kvr, kv16, sq, r1, r2, r3, wkvb, wob, qg, spt, spi, att, ot, oti,
    pboth, psend, precv, pown, ysend, yrecv, zsend, zrecv, dz,
    dat, pjf, pjs, ob, gls, gps,
    ss, rs, ls,
):
    b = lax.axis_index("batch")
    k = lax.axis_index("query")
    xlo = b // 2
    c = b % 2
    y = k // 16
    z = (k // 2) % 8
    xhi = k % 2
    swapped = c != xhi
    kept = c == xhi

    def dev(xlo_, c_, y_, z_, xhi_):
        return (xlo_ * 2 + c_, (y_ * 8 + z_) * 2 + xhi_)

    sib = dev(xlo, 1 - c, y, z, xhi)
    diag = dev(xlo, xhi, y, z, c)
    z4 = z % 4
    zt = 2 * z4 + z // 4
    zs = z // 2 + 4 * (z % 2)
    same = jnp.logical_and(kept, z == zt)

    def dev_y(j):
        return dev(xlo, c, (y + j) % 4, z, xhi)

    def dev_z(j):
        return dev(xlo, c, y, (z + j) % 8, xhi)

    def yb(j):
        return (y + 4 - j) % 4

    def zb(j):
        return (z + 8 - j) % 8

    def back_to(j, i):
        return dev(xlo, xhi, (y + j) % 4, (z + i) % 8, c)

    def on(when, fn):
        if when is None:
            fn()
        else:
            pl.when(when)(fn)

    sends, arrivals, locals_ = [], {}, {}

    def go(name, j, src, dst, to, arrive, when=None, rj=None):
        i = BASE[name] + j
        copy = pltpu.make_async_remote_copy(
            src_ref=src, dst_ref=dst, send_sem=ss.at[i],
            recv_sem=rs.at[i if rj is None else BASE[name] + rj],
            device_id=to, device_id_type=MESH,
        )
        on(when, copy.start)
        sends.append((copy, when))
        here = pltpu.make_async_remote_copy(
            src_ref=arrive, dst_ref=arrive, send_sem=ss.at[i], recv_sem=rs.at[i],
            device_id=sib, device_id_type=MESH,
        )
        arrivals[name, j] = (here, when)

    def got(name, j=0):
        here, when = arrivals.pop((name, j))
        on(when, here.wait_recv)

    def local(i, src, dst, when=None):
        copy = pltpu.make_async_copy(src, dst, ls.at[i])
        on(when, copy.start)
        locals_[i] = (copy, when)

    def got_local(i):
        copy, when = locals_.pop(i)
        on(when, copy.wait)

    def drain():
        for i in list(locals_):
            got_local(i)
        for name, j in list(arrivals):
            got(name, j)
        for copy, when in sends:
            on(when, copy.wait_send)

    barrier = pltpu.get_barrier_semaphore()
    greet = [sib, dev(xlo, 1 - c, y, z, 1 - xhi), dev(xlo, c, y, z, 1 - xhi)]
    greet += [dev_y(j) for j in (1, 2, 3)] + [dev_z(j) for j in range(1, 8)]
    greet += [back_to(j, i) for j in range(4) for i in range(8) if i in NEAR_ROWS + (6,) and (j, i) != (0, 0)]
    for to in greet:
        pl.semaphore_signal(barrier, inc=1, device_id=to, device_id_type=MESH)

    def far(a, t):
        return jnp.logical_not(jnp.logical_and(same, jnp.logical_and(xlo == a, xhi == t)))

    for a in (0, 1):
        for t in (0, 1):

            @pl.when(jnp.logical_not(jnp.logical_and(same, jnp.logical_and(xlo == a, c == t))))
            def _():
                pl.semaphore_signal(barrier, inc=1, device_id=dev(a, t, y, zt, c), device_id_type=MESH)

            @pl.when(far(a, t))
            def _():
                pl.semaphore_signal(barrier, inc=1, device_id=dev(a, xhi, y, zs, t), device_id_type=MESH)

    head = y * 4 + z4
    local(13, cot.at[0], cotb)
    local(0, wkv, wkvb)
    local(1, wo.at[pl.ds(pl.multiple_of(head * 64, 64), 64)], wob)

    kvw = kv[0].astype(F32)
    for t in (0, 1):
        kvs[t] = jnp.concatenate(
            [kvw[:, t * 1024:t * 1024 + 512], kvw[:, t * 1024 + 512:t * 1024 + 1024]], axis=0
        ).astype(BF)
    pl.semaphore_wait(barrier, len(greet) + 8 - 2 * same.astype(jnp.int32))

    mine = [jnp.logical_and(kept, c == t) for t in (0, 1)]
    other = [jnp.logical_not(m) for m in mine]
    for t in (0, 1):
        go("kvrow", t, kvs.at[t], kvr.at[xhi], dev(xlo, t, y, z, c), kvr.at[t], when=other[t], rj=xhi)
    local(2, kvs.at[c], kvr.at[xhi], when=kept)
    go("swap_q", 0, points.at[0], qb, diag, qb, when=swapped)
    local(4, points.at[0], qb, when=kept)
    sw = sqkv[0].astype(F32)
    pad = jnp.zeros((8, 64), F32)
    for h in range(16):
        top = jnp.concatenate([sw[:, h * 64:h * 64 + 64], sw[:, 1024 + h * 64:1024 + h * 64 + 64]], axis=1)
        low = jnp.concatenate([sw[:, 2048 + h * 64:2048 + h * 64 + 64], pad], axis=1)
        sq[h] = jnp.concatenate([top, low], axis=0).astype(BF)
    for j in FAR_Y:
        go("qy", j - 1, sq.at[pl.ds((y + j) % 4 * 4, 4)], r1.at[y], dev_y(j), r1.at[yb(j)])
    local(3, sq.at[pl.ds(y * 4, 4)], r1.at[y])
    hot = (lax.broadcasted_iota(jnp.int32, (256, 256), 0) == order[0]).astype(F32).astype(BF)
    got_local(13)
    gsend[...] = tn(hot, cotb[...]).astype(BF)

    go("swap_g", 0, gsend, gb, diag, gb, when=swapped)
    local(5, gsend, gb, when=kept)

    got("kvrow", 0)
    got("kvrow", 1)
    got_local(2)
    p0 = kvr[0].astype(F32)
    p1 = kvr[1].astype(F32)
    left = jnp.concatenate([p0[:8], p1[:8]], axis=0)
    right = jnp.concatenate([p0[8:], p1[8:]], axis=0)
    kv16[c, y, z] = jnp.concatenate([left, right], axis=1).astype(BF)
    for i in FAR_Y:
        go("ky", i - 1, kv16.at[c, y, z], kv16.at[c, y, z], dev_y(i), kv16.at[c, yb(i), z])
    for j in MIX_Z:
        go("kz", j - 1, kv16.at[c, y, z], kv16.at[c, y, z], dev_z(j), kv16.at[c, y, zb(j)])

    def on_along_y(j):
        got("kz", j - 1)
        slot = zb(j)
        for i in FAR_Y:
            go("ky", j * 3 + i - 1, kv16.at[c, y, slot], kv16.at[c, y, slot], dev_y(i), kv16.at[c, yb(i), slot])

    for j in ARRIVE_Z[:2]:
        on_along_y(j)

    for j in (1, 2, 3):
        got("qy", j - 1)
    got_local(3)
    for j in FAR_Z:
        go("qz", j - 1, r1.at[:, (z + j) % 4], r2.at[:, z], dev_z(j), r2.at[:, zb(j)])
    local(6, r1.at[:, z4], r2.at[:, z])

    for j in ARRIVE_Z[2:]:
        on_along_y(j)
    go("ks", 0, kv16.at[c, y], kv16.at[c, y], sib, kv16.at[1 - c, y])

    got_local(0)
    got("swap_q")
    got_local(4)
    qw = nt(qb[...], wkvb[:, 0:1024]).astype(BF)
    qg[0, 0:256] = qw[:, 0:512]
    qg[1, 0:256] = qw[:, 512:1024]

    got("swap_g")
    got_local(5)
    gw = nt(gb[...], wkvb[:, 1024:2048]).astype(BF)
    qg[0, 256:512] = gw[:, 0:512]
    qg[1, 256:512] = gw[:, 512:1024]

    for j in range(1, 8):
        got("qz", j - 1)
    got_local(6)
    for t in (0, 1):
        go("qx", t, r2, r3.at[:, :, xhi], dev(xlo, t, y, z, c), r3.at[:, :, t], when=other[t], rj=xhi)
    local(7, r2, r3.at[:, :, xhi], when=kept)

    for i in (1, 3, 2):
        for j in range(8):
            got("ky", j * 3 + i - 1)
        slot = yb(i)
        go("ks", i, kv16.at[c, slot], kv16.at[c, slot], sib, kv16.at[1 - c, slot])
    for j in range(4):
        got("ks", j)

    keys = kv16[0].reshape(512, 1024)
    values = kv16[1].reshape(512, 1024)
    scale = 1.0 / 1024 ** 0.5
    s = nt(keys, qb[...]) * scale
    e = jnp.exp(s - jnp.max(s, axis=0, keepdims=True))
    p = e / jnp.sum(e, axis=0, keepdims=True)
    dp = nt(values, gb[...])
    delta = jnp.sum(p * dp, axis=0, keepdims=True)
    ds = (p * (dp - delta) * scale).astype(BF)
    pboth[...] = jnp.concatenate([ds, p.astype(BF)], axis=1).reshape(4, 128, 512)

    for i in FAR_Y + (0,):
        yi = (y + i) % 4
        psend[yi] = nn(pboth[yi], qg[1 - c]).astype(BF).reshape(8, 16, 512)
        go("pair", i, psend.at[yi], precv.at[yi], sib, precv.at[yi])
    for i in FAR_Y + (0,):
        yi = (y + i) % 4
        pown[yi] = nn(pboth[yi], qg[c]).reshape(8, 16, 512)
    for i in FAR_Y:
        yi = (y + i) % 4
        got("pair", i)
        for j in FAR_Z + (0,):
            zj = (z + j) % 8
            ysend[j, i - 1] = (pown[yi, zj] + precv[yi, zj].astype(F32)).astype(BF)
            go("ry", j * 3 + i - 1, ysend.at[j, i - 1], yrecv.at[j, i - 1], dev_y(i), yrecv.at[j, i - 1])

    gps[...] = tn(ds, kv16[0].reshape(512, 1024)).astype(BF)
    got("qx", 0)
    got("qx", 1)
    got_local(7)
    go("pts", 0, gps, gpts.at[0], diag, gpts.at[0], when=swapped)
    local(8, gps, gpts.at[0], when=kept)
    tiles = r3[...].astype(F32).reshape(64, 16, 128)
    top = tiles[:, :8].reshape(512, 128)
    low = tiles[:, 8:].reshape(512, 128)
    sq_q = top[:, :64].astype(BF)
    sq_k = top[:, 64:].astype(BF)
    sq_v = low[:, :64].astype(BF)
    kt = top[:, 64:].T.astype(BF)
    vt = low[:, :64].T.astype(BF)

    def near_rows(ref):
        return jnp.concatenate([ref[:, (z + i) % 8, c].astype(F32) for i in NEAR_ROWS], axis=0)

    own = near_rows(r3)
    own_q = own[:, :8].reshape(128, 128)[:, :64].astype(BF)
    own_v = own[:, 8:].reshape(128, 128)[:, :64].astype(BF)
    sscale = 1.0 / 64 ** 0.5

    def columns_softmax(scores):
        weights = jnp.exp(scores - jnp.max(scores, axis=0, keepdims=True))
        return weights / jnp.sum(weights, axis=0, keepdims=True)

    def attend(probs):
        high = probs.astype(BF)
        rounded = nn(vt, high)
        return rounded, rounded + nn(vt, (probs - high.astype(F32)).astype(BF))

    sprobs = columns_softmax(nt(sq_k, sq_q) * sscale)
    spt[...] = sprobs.reshape(4, 8, 2, 8, 512)
    attended, ot[...] = attend(sprobs)
    att[...] = attended.astype(BF)
    sprobs = columns_softmax(nt(sq_k, own_q) * sscale)
    spi[...] = sprobs
    _, oti[...] = attend(sprobs)

    got("pair", 0)
    for j in FAR_Z + (0,):
        zj = (z + j) % 8
        acc = pown[y, zj] + precv[y, zj].astype(F32)
        for i in FAR_Y:
            got("ry", j * 3 + i - 1)
            acc = acc + yrecv[j, i - 1].astype(F32)
        if j:
            zsend[j - 1] = acc.astype(BF)
            go("rz", j - 1, zsend.at[j - 1], zrecv.at[j - 1], dev_z(j), zrecv.at[j - 1])
    for j in range(1, 8):
        got("rz", j - 1)
        acc = acc + zrecv[j - 1].astype(F32)
    dz[c, y, z] = acc.astype(BF)

    for j in MIX_Z:
        go("gz", j - 1, dz.at[c, y, z], dz.at[c, y, z], dev_z(j), dz.at[c, y, zb(j)])
    for i in FAR_Y:
        go("gy", i - 1, dz.at[c, y, z], dz.at[c, y, z], dev_y(i), dz.at[c, yb(i), z])
    for j in ARRIVE_Z:
        got("gz", j - 1)
        slot = zb(j)
        for i in FAR_Y:
            go("gy", j * 3 + i - 1, dz.at[c, y, slot], dz.at[c, y, slot], dev_y(i), dz.at[c, yb(i), slot])
    go("gs", 0, dz.at[c, y], dz.at[c, y], sib, dz.at[1 - c, y])
    for i in (1, 3, 2):
        for j in range(8):
            got("gy", j * 3 + i - 1)
        slot = yb(i)
        go("gs", i, dz.at[c, slot], dz.at[c, slot], sib, dz.at[1 - c, slot])
    for i in range(4):
        got("gs", i)

    got_local(1)
    dz0 = dz[0].reshape(512, 512)
    dz1 = dz[1].reshape(512, 512)
    datt = nt(dz0, wob[:, 0:512]) + nt(dz1, wob[:, 512:1024])
    datt = datt.astype(BF)
    dattw = datt.astype(F32)
    dat[...] = dattw.reshape(4, 8, 2, 8, 64)
    own_datt = near_rows(dat).reshape(128, 64)
    sdelta = jnp.sum(dattw.T * ot[...], axis=0, keepdims=True)
    own_sdelta = jnp.sum(own_datt.T * oti[...], axis=0, keepdims=True)
    rows_p = near_rows(spt).reshape(128, 512)
    sds = (rows_p * (nt(own_v, datt) - sdelta) * sscale).astype(BF)
    dk = nn(sds, sq_q)
    dv = nn(rows_p.astype(BF), datt)
    sds = (spi[...] * (nt(sq_v, own_datt.astype(BF)) - own_sdelta) * sscale).astype(BF)
    dq = nn(kt, sds).T
    m1 = jnp.concatenate([dq, dk], axis=1).reshape(16, 8, 128)
    m2 = jnp.concatenate([dv, jnp.zeros((128, 64), F32)], axis=1).reshape(16, 8, 128)
    ob[...] = jnp.concatenate([m1, m2], axis=1).astype(BF).reshape(4, 4, 16, 128)

    for at, i in reversed(list(enumerate(NEAR_ROWS))):
        for j in (2, 1, 3, 0):
            go("back", j * 4 + at, ob.at[at, (y + j) % 4], or2.at[y, z4], back_to(j, i),
               or2.at[yb(j), (z + 8 - i) % 4], when=None if j + i else swapped)
    local(11, ob.at[0, y], or2.at[y, z4], when=kept)

    pjf[:, 0:512] = nn(att[...], dz0)
    pjf[:, 512:1024] = nn(att[...], dz1)
    pjs[...] = pjf[pl.ds(pl.multiple_of((z // 4 * 2 + c) * 16, 16), 16), :].astype(BF)
    shape_at = xlo * 2 + xhi
    for a in (0, 1):
        for t in (0, 1):
            away = jnp.logical_not(jnp.logical_and(same, jnp.logical_and(xlo == a, c == t)))
            go("proj", a * 2 + t, pjs, pjr.at[shape_at], dev(a, t, y, zt, c), pjr.at[a * 2 + t], when=away, rj=shape_at)
    local(9, pjs, pjr.at[shape_at], when=same)

    rows = [dz[t, y, z].astype(F32) for t in (0, 1)]
    first = c == 0
    gls[...] = jnp.concatenate([jnp.where(first, r[:8], r[8:]) for r in rows], axis=0).astype(BF)
    go("lat", 0, gls, glr, diag, glr, when=swapped)
    local(10, gls, glr, when=kept)
    drain()


def finish(pts, or2, glr, pjr, gpts, glat, gqkv, gproj, held, sem):
    into = pltpu.make_async_copy(pts, held, sem.at[0])
    into.start()
    into.wait()
    out = pltpu.make_async_copy(held, gpts, sem.at[1])
    out.start()
    total = pjr[0].astype(F32)
    for src in (1, 2, 3):
        total = total + pjr[src].astype(F32)
    gproj[...] = total
    lr = glr[...].astype(F32)
    glat[0] = jnp.concatenate([lr[:8], lr[8:]], axis=1).astype(BF)
    res = or2[...].astype(F32).reshape(16, 16, 128)
    parts = [res[h, :8, 0:64] for h in range(16)]
    parts += [res[h, :8, 64:128] for h in range(16)]
    parts += [res[h, 8:, 0:64] for h in range(16)]
    gqkv[0] = jnp.concatenate(parts, axis=1).astype(BF)
    out.wait()


def on_device(points, order, cotangent, kv_cross, self_qkv, kv_weight, out_weight):
    vmem = pl.BlockSpec(memory_space=pltpu.VMEM)
    hbm = pl.BlockSpec(memory_space=pl.ANY)
    scratch = [
        ((256, 1024), BF),
        ((256, 1024), BF),
        ((256, 1024), BF),
        ((256, 1024), BF),
        ((2, 16, 512), BF),
        ((2, 16, 512), BF),
        ((2, 4, 8, 16, 1024), BF),
        ((16, 16, 128), BF),
        ((4, 4, 16, 128), BF),
        ((4, 8, 16, 128), BF),
        ((4, 8, 2, 16, 128), BF),
        ((1024, 2048), BF),
        ((64, 1024), BF),
        ((2, 512, 512), BF),
        ((4, 8, 2, 8, 512), F32),
        ((512, 128), F32),
        ((64, 512), BF),
        ((64, 512), F32),
        ((64, 128), F32),
        ((4, 128, 512), BF),
        ((4, 8, 16, 512), BF),
        ((4, 8, 16, 512), BF),
        ((4, 8, 16, 512), F32),
        ((8, 3, 16, 512), BF),
        ((8, 3, 16, 512), BF),
        ((7, 16, 512), BF),
        ((7, 16, 512), BF),
        ((2, 4, 8, 16, 512), BF),
        ((4, 8, 2, 8, 64), F32),
        ((64, 1024), F32),
        ((16, 1024), BF),
        ((4, 4, 16, 128), BF),
        ((16, 512), BF),
        ((256, 1024), BF),
    ]
    parts = pl.pallas_call(
        kernel,
        out_shape=(
            jax.ShapeDtypeStruct((1, 256, 1024), BF),
            jax.ShapeDtypeStruct((4, 4, 16, 128), BF),
            jax.ShapeDtypeStruct((16, 512), BF),
            jax.ShapeDtypeStruct((4, 16, 1024), BF),
        ),
        in_specs=[hbm, vmem, hbm, vmem, vmem, hbm, hbm],
        out_specs=(hbm, hbm, hbm, hbm),
        scratch_shapes=[pltpu.VMEM(shape, dtype) for shape, dtype in scratch]
        + [pltpu.SemaphoreType.DMA((COUNT,)), pltpu.SemaphoreType.DMA((COUNT,)), pltpu.SemaphoreType.DMA((14,))],
        name="fused_backward",
        cost_estimate=pl.CostEstimate(flops=3_000_000_000, bytes_accessed=8_000_000, transcendentals=400_000),
        compiler_params=pltpu.CompilerParams(
            collective_id=0, has_side_effects=True, vmem_limit_bytes=56 * 1024 * 1024
        ),
    )(points, order, cotangent, kv_cross, self_qkv, kv_weight, out_weight)
    return pl.pallas_call(
        finish,
        out_shape=(
            jax.ShapeDtypeStruct((1, 256, 1024), BF),
            jax.ShapeDtypeStruct((1, 8, 1024), BF),
            jax.ShapeDtypeStruct((1, 8, 3072), BF),
            jax.ShapeDtypeStruct((16, 1024), F32),
        ),
        in_specs=[hbm, vmem, vmem, vmem],
        out_specs=(hbm, vmem, vmem, vmem),
        scratch_shapes=[pltpu.VMEM((1, 256, 1024), BF), pltpu.SemaphoreType.DMA((2,))],
        name="finish",
        cost_estimate=pl.CostEstimate(flops=100_000, bytes_accessed=1_500_000, transcendentals=0),
    )(*parts)


def solution(mesh):
    rows = P("batch", "query", None)
    return jax.shard_map(
        on_device,
        mesh=mesh,
        in_specs=(rows, rows, rows, rows, rows, P(), P()),
        out_specs=(rows, rows, rows, P("query", None)),
        check_vma=False,
    )
```

```python
import functools

import jax
import jax.numpy as jnp
from jax import lax
from jax.experimental import pallas as pl
from jax.experimental.pallas import tpu as pltpu
from jax.sharding import PartitionSpec as P

MESH = pl.DeviceIdType.MESH
BF = jnp.bfloat16
F32 = jnp.float32


def nt(a, b):
    return lax.dot_general(a, b, (((1,), (1,)), ((), ())), preferred_element_type=F32)


def nn(a, b):
    return lax.dot_general(a, b, (((1,), (0,)), ((), ())), preferred_element_type=F32)


def tn(a, b):
    return lax.dot_general(a, b, (((0,), (0,)), ((), ())), preferred_element_type=F32)


GROUPS = dict(
    kvrow=2, qy=3, qz=7, qx=2, swap_q=1, swap_g=1, kz=7, ky=3, ks=1, kyb=3, kzb=7, ksb=1,
    pair=4, ry=24, rz=7, gz=7, gy=24, gs=4, lat=1, proj=4, back=16, pts=1,
)
KA, KB = 768, 256
MIX_Z = (4, 1, 7, 2, 6, 3, 5)
FAR_Z = (4, 3, 5, 2, 6, 1, 7)
NEAR_Z = (1, 7, 2, 6, 3, 5, 4)
ARRIVE_Z = (1, 7, 2, 6, 4, 3, 5)
FAR_Y = (2, 1, 3)
NEAR_ROWS = (0, 1, 7, 2)
BASE = {}
COUNT = 0
for _name, _n in GROUPS.items():
    BASE[_name] = COUNT
    COUNT += _n


def kernel(
    points, order_in, cot, kv_in, sqkv_in, wkv, wo,
    gpts, or2, glr, pjr,
    order, kv, sqkv, cotb, gsend, qgb, kvs, kvr, kv16, kvb, sq, r1, r2, r3, wkvb, wob, qg, spt, spi, att, ot, oti,
    pboth, psend, precv, pown, ysend, yrecv, zsend, zrecv, dz,
    dat, pjf, pjs, ob, gls, gps,
    ss, rs, ls,
):
    b = lax.axis_index("batch")
    k = lax.axis_index("query")
    xlo = b // 2
    c = b % 2
    y = k // 16
    z = (k // 2) % 8
    xhi = k % 2
    swapped = c != xhi
    kept = c == xhi

    def dev(xlo_, c_, y_, z_, xhi_):
        return (xlo_ * 2 + c_, (y_ * 8 + z_) * 2 + xhi_)

    sib = dev(xlo, 1 - c, y, z, xhi)
    diag = dev(xlo, xhi, y, z, c)
    z4 = z % 4
    zt = 2 * z4 + z // 4
    zs = z // 2 + 4 * (z % 2)
    same = jnp.logical_and(kept, z == zt)

    def dev_y(j):
        return dev(xlo, c, (y + j) % 4, z, xhi)

    def dev_z(j):
        return dev(xlo, c, y, (z + j) % 8, xhi)

    def yb(j):
        return (y + 4 - j) % 4

    def zb(j):
        return (z + 8 - j) % 8

    def back_to(j, i):
        return dev(xlo, xhi, (y + j) % 4, (z + i) % 8, c)

    def on(when, fn):
        if when is None:
            fn()
        else:
            pl.when(when)(fn)

    sends, arrivals, locals_ = [], {}, {}

    def go(name, j, src, dst, to, arrive, when=None, rj=None, together=False):
        i = BASE[name] + j
        copy = pltpu.make_async_remote_copy(
            src_ref=src, dst_ref=dst, send_sem=ss.at[BASE[name] if together else i],
            recv_sem=rs.at[i if rj is None else BASE[name] + rj],
            device_id=to, device_id_type=MESH,
        )
        on(when, copy.start)
        if not together:
            sends.append((copy, when))
        if arrive is not None:
            all_here(name, j, arrive, when)

    def all_here(name, j, arrive, when=None):
        i = BASE[name] + j
        here = pltpu.make_async_remote_copy(
            src_ref=arrive, dst_ref=arrive, send_sem=ss.at[i], recv_sem=rs.at[i],
            device_id=sib, device_id_type=MESH,
        )
        arrivals[name, j] = (here, when)

    def all_sent(name, total):
        i = BASE[name]
        copy = pltpu.make_async_remote_copy(
            src_ref=total, dst_ref=total, send_sem=ss.at[i], recv_sem=rs.at[i],
            device_id=sib, device_id_type=MESH,
        )
        sends.append((copy, None))

    def got(name, j=0):
        here, when = arrivals.pop((name, j))
        on(when, here.wait_recv)

    def local(i, src, dst, when=None):
        copy = pltpu.make_async_copy(src, dst, ls.at[i])
        on(when, copy.start)
        locals_[i] = (copy, when)

    def got_local(i):
        copy, when = locals_.pop(i)
        on(when, copy.wait)

    def drain():
        for i in list(locals_):
            got_local(i)
        for name, j in list(arrivals):
            got(name, j)
        leave()

    def leave():
        for copy, when in sends:
            on(when, copy.wait_send)
        sends.clear()

    barrier = pltpu.get_barrier_semaphore()
    greet = [sib, dev(xlo, 1 - c, y, z, 1 - xhi), dev(xlo, c, y, z, 1 - xhi)]
    greet += [dev_y(j) for j in (1, 2, 3)] + [dev_z(j) for j in range(1, 8)]
    greet += [back_to(j, i) for j in range(4) for i in range(8) if i in NEAR_ROWS + (6,) and (j, i) != (0, 0)]
    for to in greet:
        pl.semaphore_signal(barrier, inc=1, device_id=to, device_id_type=MESH)

    def far(a, t):
        return jnp.logical_not(jnp.logical_and(same, jnp.logical_and(xlo == a, xhi == t)))

    for a in (0, 1):
        for t in (0, 1):

            @pl.when(jnp.logical_not(jnp.logical_and(same, jnp.logical_and(xlo == a, c == t))))
            def _():
                pl.semaphore_signal(barrier, inc=1, device_id=dev(a, t, y, zt, c), device_id_type=MESH)

            @pl.when(far(a, t))
            def _():
                pl.semaphore_signal(barrier, inc=1, device_id=dev(a, xhi, y, zs, t), device_id_type=MESH)

    local(14, kv_in, kv)
    local(15, sqkv_in, sqkv)
    local(16, order_in, order)
    head = y * 4 + z4
    local(13, cot.at[0], cotb)
    local(0, wkv, wkvb)
    local(1, wo.at[pl.ds(pl.multiple_of(head * 64, 64), 64)], wob)

    got_local(14)
    kvw = kv[0].astype(F32)
    for t in (0, 1):
        kvs[t] = jnp.concatenate(
            [kvw[:, t * 1024:t * 1024 + 512], kvw[:, t * 1024 + 512:t * 1024 + 1024]], axis=0
        ).astype(BF)
    pl.semaphore_wait(barrier, len(greet) + 8 - 2 * same.astype(jnp.int32))

    mine = [jnp.logical_and(kept, c == t) for t in (0, 1)]
    other = [jnp.logical_not(m) for m in mine]
    for t in (0, 1):
        go("kvrow", t, kvs.at[t], kvr.at[xhi], dev(xlo, t, y, z, c), kvr.at[t], when=other[t], rj=xhi)
    local(2, kvs.at[c], kvr.at[xhi], when=kept)
    go("swap_q", 0, points.at[0], qgb.at[0], diag, qgb.at[0], when=swapped)
    local(4, points.at[0], qgb.at[0], when=kept)
    got_local(15)
    sw = sqkv[0].astype(F32)
    pad = jnp.zeros((8, 64), F32)
    for h in range(16):
        top = jnp.concatenate([sw[:, h * 64:h * 64 + 64], sw[:, 1024 + h * 64:1024 + h * 64 + 64]], axis=1)
        low = jnp.concatenate([sw[:, 2048 + h * 64:2048 + h * 64 + 64], pad], axis=1)
        sq[h] = jnp.concatenate([top, low], axis=0).astype(BF)
    for j in FAR_Y:
        go("qy", j - 1, sq.at[pl.ds((y + j) % 4 * 4, 4)], r1.at[y], dev_y(j), None, rj=0, together=True)
    all_here("qy", 0, r1.at[pl.ds(0, 3)])
    all_sent("qy", r1.at[pl.ds(0, 3)])
    local(3, sq.at[pl.ds(y * 4, 4)], r1.at[y])
    got_local(16)
    hot = (lax.broadcasted_iota(jnp.int32, (256, 256), 0) == order[0]).astype(F32).astype(BF)
    got_local(13)
    gsend[...] = tn(hot, cotb[...]).astype(BF)

    go("swap_g", 0, gsend, qgb.at[1], diag, qgb.at[1], when=swapped)
    local(5, gsend, qgb.at[1], when=kept)

    got("kvrow", 0)
    got("kvrow", 1)
    got_local(2)
    p0 = kvr[0].astype(F32)
    p1 = kvr[1].astype(F32)
    left = jnp.concatenate([p0[:8], p1[:8]], axis=0)
    right = jnp.concatenate([p0[8:], p1[8:]], axis=0)
    kv16[c, y, z] = jnp.concatenate([left, right[:, :KA - 512]], axis=1).astype(BF)
    kvb[c, y, z] = right[:, KA - 512:].astype(BF)
    for i in FAR_Y:
        go("ky", i - 1, kv16.at[c, y, z], kv16.at[c, y, z], dev_y(i), None, together=True)
    for j in MIX_Z:
        go("kz", j - 1, kv16.at[c, y, z], kv16.at[c, y, z], dev_z(j), kv16.at[c, y, zb(j)], together=True)
    all_sent("kz", kv16.at[0, 0, pl.ds(0, 7)])

    def on_along_y(j):
        got("kz", j - 1)
        slot = zb(j)
        for i in FAR_Y:
            go("ky", i - 1, kv16.at[c, y, slot], kv16.at[c, y, slot], dev_y(i), None, together=True)

    for i in FAR_Y:
        go("kyb", i - 1, kvb.at[c, y, z], kvb.at[c, y, z], dev_y(i), kvb.at[c, yb(i), z], together=True)
    all_sent("kyb", kvb.at[0, 0, pl.ds(0, 3)])
    for j in ARRIVE_Z[:4]:
        on_along_y(j)
    for j in (1, 2, 3):
        got("kyb", j - 1)
    for j in FAR_Z:
        go("kzb", j - 1, kvb.at[c, :, z], kvb.at[c, :, z], dev_z(j), None, rj=0, together=True)
    all_here("kzb", 0, kvb.at[c, :, pl.ds(0, 7)])
    all_sent("kzb", kvb.at[c, :, pl.ds(0, 7)])
    for j in ARRIVE_Z[4:]:
        on_along_y(j)
    got("qy")
    got_local(3)
    for j in FAR_Z:
        go("qz", j - 1, r1.at[:, (z + j) % 4], r2.at[:, z], dev_z(j), None, rj=0, together=True)
    all_here("qz", 0, r2.at[:, pl.ds(0, 7)])
    all_sent("qz", r2.at[:, pl.ds(0, 7)])
    local(6, r1.at[:, z4], r2.at[:, z])

    all_sent("ky", kv16.at[0, pl.ds(0, 3)])
    go("ks", 0, kv16.at[c, y], kv16.at[c, y], sib, None, together=True)

    got_local(0)
    got("swap_q")
    got_local(4)
    qw = nt(qgb[0], wkvb[:, 0:1024]).astype(BF)
    qg[0, 0:256] = qw[:, 0:512]
    qg[1, 0:256] = qw[:, 512:1024]

    got("swap_g")
    got_local(5)
    gw = nt(qgb[1], wkvb[:, 1024:2048]).astype(BF)
    qg[0, 256:512] = gw[:, 0:512]
    qg[1, 256:512] = gw[:, 512:1024]

    got("kzb")
    go("ksb", 0, kvb.at[c], kvb.at[c], sib, kvb.at[1 - c])
    for i in (1, 3, 2):
        slot = yb(i)
        all_here("ky", i - 1, kv16.at[c, slot])
        got("ky", i - 1)
        go("ks", 0, kv16.at[c, slot], kv16.at[c, slot], sib, None, together=True)
    all_here("ks", 0, kv16.at[1 - c])
    all_sent("ks", kv16.at[c])
    got("qz")
    got_local(6)
    for t in (0, 1):
        go("qx", t, r2, r3.at[:, :, xhi], dev(xlo, t, y, z, c), r3.at[:, :, t], when=other[t], rj=xhi)
    local(7, r2, r3.at[:, :, xhi], when=kept)

    def product(t):
        return nt(kv16[t].reshape(512, KA), qgb[t, :, 0:KA]) + nt(kvb[t].reshape(512, KB), qgb[t, :, KA:1024])

    mine_first = product(c)
    got("ksb")
    got("ks")
    then = product(1 - c)
    scale = 1.0 / 1024 ** 0.5
    s = jnp.where(c == 0, mine_first, then) * scale
    e = jnp.exp(s - jnp.max(s, axis=0, keepdims=True))
    p = e / jnp.sum(e, axis=0, keepdims=True)
    dp = jnp.where(c == 0, then, mine_first)
    delta = jnp.sum(p * dp, axis=0, keepdims=True)
    ds = (p * (dp - delta) * scale).astype(BF)
    pboth[...] = jnp.concatenate([ds, p.astype(BF)], axis=1).reshape(4, 128, 512)

    for i in FAR_Y + (0,):
        yi = (y + i) % 4
        psend[yi] = nn(pboth[yi], qg[1 - c]).astype(BF).reshape(8, 16, 512)
        go("pair", i, psend.at[yi], precv.at[yi], sib, precv.at[yi], together=True)
    for i in FAR_Y + (0,):
        yi = (y + i) % 4
        pown[yi] = nn(pboth[yi], qg[c]).reshape(8, 16, 512)
    all_sent("pair", psend)
    for i in FAR_Y:
        yi = (y + i) % 4
        got("pair", i)
        for j in FAR_Z + (0,):
            zj = (z + j) % 8
            ysend[j, i - 1] = (pown[yi, zj] + precv[yi, zj].astype(F32)).astype(BF)
            go("ry", j * 3 + i - 1, ysend.at[j, i - 1], yrecv.at[j, i - 1], dev_y(i), yrecv.at[j, i - 1], together=True)
    all_sent("ry", ysend)

    gps[:, 0:KA] = tn(ds, kv16[0].reshape(512, KA)).astype(BF)
    gps[:, KA:1024] = tn(ds, kvb[0].reshape(512, KB)).astype(BF)
    go("pts", 0, gps, gpts.at[0], diag, gpts.at[0], when=swapped)
    local(8, gps, gpts.at[0], when=kept)
    got("pair", 0)
    for j in FAR_Z + (0,):
        zj = (z + j) % 8
        acc = pown[y, zj] + precv[y, zj].astype(F32)
        for i in FAR_Y:
            got("ry", j * 3 + i - 1)
            acc = acc + yrecv[j, i - 1].astype(F32)
        if j:
            zsend[j - 1] = acc.astype(BF)
            go("rz", j - 1, zsend.at[j - 1], zrecv.at[j - 1], dev_z(j), None, rj=0, together=True)
    all_here("rz", 0, zrecv)
    all_sent("rz", zsend)
    got("rz")
    for j in range(1, 8):
        acc = acc + zrecv[j - 1].astype(F32)
    dz[c, y, z] = acc.astype(BF)

    for j in MIX_Z:
        go("gz", j - 1, dz.at[c, y, z], dz.at[c, y, z], dev_z(j), dz.at[c, y, zb(j)], together=True)
    all_sent("gz", dz.at[0, 0, pl.ds(0, 7)])
    for i in FAR_Y:
        go("gy", i - 1, dz.at[c, y, z], dz.at[c, y, z], dev_y(i), None, together=True)
    got("qx", 0)
    got("qx", 1)
    got_local(7)
    tiles = r3[...].astype(F32).reshape(64, 16, 128)
    top = tiles[:, :8].reshape(512, 128)
    low = tiles[:, 8:].reshape(512, 128)
    sq_q = top[:, :64].astype(BF)
    sq_k = top[:, 64:].astype(BF)
    sq_v = low[:, :64].astype(BF)
    kt = top[:, 64:].T.astype(BF)
    vt = low[:, :64].T.astype(BF)

    def near_rows(ref):
        return jnp.concatenate([ref[:, (z + i) % 8, c].astype(F32) for i in NEAR_ROWS], axis=0)

    own = near_rows(r3)
    own_q = own[:, :8].reshape(128, 128)[:, :64].astype(BF)
    own_v = own[:, 8:].reshape(128, 128)[:, :64].astype(BF)
    sscale = 1.0 / 64 ** 0.5

    def columns_softmax(scores):
        weights = jnp.exp(scores - jnp.max(scores, axis=0, keepdims=True))
        return weights / jnp.sum(weights, axis=0, keepdims=True)

    def attend(probs):
        high = probs.astype(BF)
        rounded = nn(vt, high)
        return rounded, rounded + nn(vt, (probs - high.astype(F32)).astype(BF))

    sprobs = columns_softmax(nt(sq_k, sq_q) * sscale)
    spt[...] = sprobs.reshape(4, 8, 2, 8, 512)
    attended, ot[...] = attend(sprobs)
    att[...] = attended.astype(BF)
    sprobs = columns_softmax(nt(sq_k, own_q) * sscale)
    spi[...] = sprobs
    _, oti[...] = attend(sprobs)

    for j in ARRIVE_Z:
        got("gz", j - 1)
        slot = zb(j)
        for i in FAR_Y:
            go("gy", i - 1, dz.at[c, y, slot], dz.at[c, y, slot], dev_y(i), None, together=True)
    all_sent("gy", dz.at[0, pl.ds(0, 3)])
    go("gs", 0, dz.at[c, y], dz.at[c, y], sib, None, together=True)
    for i in (1, 3, 2):
        slot = yb(i)
        all_here("gy", i - 1, dz.at[c, slot])
        got("gy", i - 1)
        go("gs", 0, dz.at[c, slot], dz.at[c, slot], sib, None, together=True)
    all_here("gs", 0, dz.at[1 - c])
    all_sent("gs", dz.at[c])
    got("gs")

    got_local(1)
    dz0 = dz[0].reshape(512, 512)
    dz1 = dz[1].reshape(512, 512)
    datt = nt(dz0, wob[:, 0:512]) + nt(dz1, wob[:, 512:1024])
    datt = datt.astype(BF)
    dattw = datt.astype(F32)
    dat[...] = dattw.reshape(4, 8, 2, 8, 64)
    own_datt = near_rows(dat).reshape(128, 64)
    sdelta = jnp.sum(dattw.T * ot[...], axis=0, keepdims=True)
    own_sdelta = jnp.sum(own_datt.T * oti[...], axis=0, keepdims=True)
    rows_p = near_rows(spt).reshape(128, 512)
    sds = (rows_p * (nt(own_v, datt) - sdelta) * sscale).astype(BF)
    dk = nn(sds, sq_q)
    dv = nn(rows_p.astype(BF), datt)
    sds = (spi[...] * (nt(sq_v, own_datt.astype(BF)) - own_sdelta) * sscale).astype(BF)
    dq = nn(kt, sds).T
    m1 = jnp.concatenate([dq, dk], axis=1).reshape(16, 8, 128)
    m2 = jnp.concatenate([dv, jnp.zeros((128, 64), F32)], axis=1).reshape(16, 8, 128)
    ob[...] = jnp.concatenate([m1, m2], axis=1).astype(BF).reshape(4, 4, 16, 128)

    for at, i in reversed(list(enumerate(NEAR_ROWS))):
        for j in (2, 1, 3, 0):
            go("back", j * 4 + at, ob.at[at, (y + j) % 4], or2.at[y, z4], back_to(j, i),
               or2.at[yb(j), (z + 8 - i) % 4], when=None if j + i else swapped)
    local(11, ob.at[0, y], or2.at[y, z4], when=kept)

    pjf[:, 0:512] = nn(att[...], dz0)
    pjf[:, 512:1024] = nn(att[...], dz1)
    pjs[...] = pjf[pl.ds(pl.multiple_of((z // 4 * 2 + c) * 16, 16), 16), :].astype(BF)
    shape_at = xlo * 2 + xhi
    for a in (0, 1):
        for t in (0, 1):
            away = jnp.logical_not(jnp.logical_and(same, jnp.logical_and(xlo == a, c == t)))
            go("proj", a * 2 + t, pjs, pjr.at[shape_at], dev(a, t, y, zt, c), pjr.at[a * 2 + t], when=away, rj=shape_at)
    local(9, pjs, pjr.at[shape_at], when=same)

    rows = [dz[t, y, z].astype(F32) for t in (0, 1)]
    first = c == 0
    gls[...] = jnp.concatenate([jnp.where(first, r[:8], r[8:]) for r in rows], axis=0).astype(BF)
    go("lat", 0, gls, glr, diag, glr, when=swapped)
    local(10, gls, glr, when=kept)
    leave()
    drain()


def finish(pts_in, or2_in, glr_in, pjr_in, gpts_out, glat_out, gqkv_out, gproj_out,
           pts, or2, glr, pjr, glat, gqkv, gproj, sem):
    def copy(i, src, dst):
        moved = pltpu.make_async_copy(src, dst, sem.at[i])
        moved.start()
        return moved

    loads = [copy(0, pts_in, pts), copy(1, pjr_in, pjr), copy(2, glr_in, glr), copy(3, or2_in, or2)]
    loads[0].wait()
    stores = [copy(4, pts, gpts_out)]
    loads[1].wait()
    total = pjr[0].astype(F32)
    for src in (1, 2, 3):
        total = total + pjr[src].astype(F32)
    gproj[...] = total
    stores.append(copy(5, gproj, gproj_out))
    loads[2].wait()
    lr = glr[...].astype(F32)
    glat[0] = jnp.concatenate([lr[:8], lr[8:]], axis=1).astype(BF)
    stores.append(copy(6, glat, glat_out))
    loads[3].wait()
    res = or2[...].astype(F32).reshape(16, 16, 128)
    parts = [res[h, :8, 0:64] for h in range(16)]
    parts += [res[h, :8, 64:128] for h in range(16)]
    parts += [res[h, 8:, 0:64] for h in range(16)]
    gqkv[0] = jnp.concatenate(parts, axis=1).astype(BF)
    stores.append(copy(7, gqkv, gqkv_out))
    for moved in stores:
        moved.wait()


def on_device(points, order, cotangent, kv_cross, self_qkv, kv_weight, out_weight):
    hbm = pl.BlockSpec(memory_space=pl.ANY)
    scratch = [
        ((1, 1, 256), jnp.int32),
        ((1, 8, 2048), BF),
        ((1, 8, 3072), BF),
        ((256, 1024), BF),
        ((256, 1024), BF),
        ((2, 256, 1024), BF),
        ((2, 16, 512), BF),
        ((2, 16, 512), BF),
        ((2, 4, 8, 16, KA), BF),
        ((2, 4, 8, 16, KB), BF),
        ((16, 16, 128), BF),
        ((4, 4, 16, 128), BF),
        ((4, 8, 16, 128), BF),
        ((4, 8, 2, 16, 128), BF),
        ((1024, 2048), BF),
        ((64, 1024), BF),
        ((2, 512, 512), BF),
        ((4, 8, 2, 8, 512), F32),
        ((512, 128), F32),
        ((64, 512), BF),
        ((64, 512), F32),
        ((64, 128), F32),
        ((4, 128, 512), BF),
        ((4, 8, 16, 512), BF),
        ((4, 8, 16, 512), BF),
        ((4, 8, 16, 512), F32),
        ((8, 3, 16, 512), BF),
        ((8, 3, 16, 512), BF),
        ((7, 16, 512), BF),
        ((7, 16, 512), BF),
        ((2, 4, 8, 16, 512), BF),
        ((4, 8, 2, 8, 64), F32),
        ((64, 1024), F32),
        ((16, 1024), BF),
        ((4, 4, 16, 128), BF),
        ((16, 512), BF),
        ((256, 1024), BF),
    ]
    parts = pl.pallas_call(
        kernel,
        out_shape=(
            jax.ShapeDtypeStruct((1, 256, 1024), BF),
            jax.ShapeDtypeStruct((4, 4, 16, 128), BF),
            jax.ShapeDtypeStruct((16, 512), BF),
            jax.ShapeDtypeStruct((4, 16, 1024), BF),
        ),
        in_specs=[hbm] * 7,
        out_specs=(hbm, hbm, hbm, hbm),
        scratch_shapes=[pltpu.VMEM(shape, dtype) for shape, dtype in scratch]
        + [pltpu.SemaphoreType.DMA((COUNT,)), pltpu.SemaphoreType.DMA((COUNT,)), pltpu.SemaphoreType.DMA((17,))],
        name="fused_backward",
        cost_estimate=pl.CostEstimate(flops=3_000_000_000, bytes_accessed=8_000_000, transcendentals=400_000),
        compiler_params=pltpu.CompilerParams(
            collective_id=0, has_side_effects=True, vmem_limit_bytes=56 * 1024 * 1024
        ),
    )(points, order, cotangent, kv_cross, self_qkv, kv_weight, out_weight)
    return pl.pallas_call(
        finish,
        out_shape=(
            jax.ShapeDtypeStruct((1, 256, 1024), BF),
            jax.ShapeDtypeStruct((1, 8, 1024), BF),
            jax.ShapeDtypeStruct((1, 8, 3072), BF),
            jax.ShapeDtypeStruct((16, 1024), F32),
        ),
        in_specs=[hbm] * 4,
        out_specs=(hbm,) * 4,
        scratch_shapes=[
            pltpu.VMEM((1, 256, 1024), BF),
            pltpu.VMEM((4, 4, 16, 128), BF),
            pltpu.VMEM((16, 512), BF),
            pltpu.VMEM((4, 16, 1024), BF),
            pltpu.VMEM((1, 8, 1024), BF),
            pltpu.VMEM((1, 8, 3072), BF),
            pltpu.VMEM((16, 1024), F32),
            pltpu.SemaphoreType.DMA((8,)),
        ],
        name="finish",
        cost_estimate=pl.CostEstimate(flops=100_000, bytes_accessed=1_500_000, transcendentals=0),
    )(*parts)


def solution(mesh):
    rows = P("batch", "query", None)
    return jax.shard_map(
        on_device,
        mesh=mesh,
        in_specs=(rows, rows, rows, rows, rows, P(), P()),
        out_specs=(rows, rows, rows, P("query", None)),
        check_vma=False,
    )
```

```python
import functools

import jax
import jax.numpy as jnp
from jax import lax
from jax.experimental import pallas as pl
from jax.experimental.pallas import tpu as pltpu
from jax.sharding import PartitionSpec as P

MESH = pl.DeviceIdType.MESH
BF = jnp.bfloat16
F32 = jnp.float32


def nt(a, b):
    return lax.dot_general(a, b, (((1,), (1,)), ((), ())), preferred_element_type=F32)


def nn(a, b):
    return lax.dot_general(a, b, (((1,), (0,)), ((), ())), preferred_element_type=F32)


def tn(a, b):
    return lax.dot_general(a, b, (((0,), (0,)), ((), ())), preferred_element_type=F32)


GROUPS = dict(
    kvrow=2, qy=3, qz=7, qx=2, swap_q=1, swap_g=1, kz=7, ky=3, ks=1, kyb=3, kzb=7, ksb=1,
    pair=4, ry=24, rz=7, gz=7, gy=24, gs=4, lat=1, proj=4, back=16, pts=1,
)
KA, KB = 896, 128
MIX_Z = (4, 1, 7, 2, 6, 3, 5)
FAR_Z = (4, 3, 5, 2, 6, 1, 7)
NEAR_Z = (1, 7, 2, 6, 3, 5, 4)
ARRIVE_Z = (1, 7, 2, 6, 4, 3, 5)
FAR_Y = (2, 1, 3)
NEAR_ROWS = (0, 1, 7, 2)
BASE = {}
COUNT = 0
for _name, _n in GROUPS.items():
    BASE[_name] = COUNT
    COUNT += _n


def kernel(
    points, order_in, cot, kv_in, sqkv_in, wkv, wo,
    gpts, or2, glr, pjr,
    order, kv, sqkv, cotb, gsend, qgb, kvs, kvr, kv16, kvb, sq, r1, r2, r3, wkvb, wob, qg, spt, spi, att, ot, oti,
    pboth, psend, precv, pown, ysend, yrecv, zsend, zrecv, dz,
    dat, pjf, pjs, ob, gls, gps,
    ss, rs, ls,
):
    b = lax.axis_index("batch")
    k = lax.axis_index("query")
    xlo = b // 2
    c = b % 2
    y = k // 16
    z = (k // 2) % 8
    xhi = k % 2
    swapped = c != xhi
    kept = c == xhi

    def dev(xlo_, c_, y_, z_, xhi_):
        return (xlo_ * 2 + c_, (y_ * 8 + z_) * 2 + xhi_)

    sib = dev(xlo, 1 - c, y, z, xhi)
    diag = dev(xlo, xhi, y, z, c)
    z4 = z % 4
    zt = 2 * z4 + z // 4
    zs = z // 2 + 4 * (z % 2)
    same = jnp.logical_and(kept, z == zt)

    def dev_y(j):
        return dev(xlo, c, (y + j) % 4, z, xhi)

    def dev_z(j):
        return dev(xlo, c, y, (z + j) % 8, xhi)

    def yb(j):
        return (y + 4 - j) % 4

    def zb(j):
        return (z + 8 - j) % 8

    def back_to(j, i):
        return dev(xlo, xhi, (y + j) % 4, (z + i) % 8, c)

    def on(when, fn):
        if when is None:
            fn()
        else:
            pl.when(when)(fn)

    sends, arrivals, locals_ = [], {}, {}

    def go(name, j, src, dst, to, arrive, when=None, rj=None, together=False):
        i = BASE[name] + j
        copy = pltpu.make_async_remote_copy(
            src_ref=src, dst_ref=dst, send_sem=ss.at[BASE[name] if together else i],
            recv_sem=rs.at[i if rj is None else BASE[name] + rj],
            device_id=to, device_id_type=MESH,
        )
        on(when, copy.start)
        if not together:
            sends.append((copy, when))
        if arrive is not None:
            all_here(name, j, arrive, when)

    def all_here(name, j, arrive, when=None):
        i = BASE[name] + j
        here = pltpu.make_async_remote_copy(
            src_ref=arrive, dst_ref=arrive, send_sem=ss.at[i], recv_sem=rs.at[i],
            device_id=sib, device_id_type=MESH,
        )
        arrivals[name, j] = (here, when)

    def all_sent(name, total):
        i = BASE[name]
        copy = pltpu.make_async_remote_copy(
            src_ref=total, dst_ref=total, send_sem=ss.at[i], recv_sem=rs.at[i],
            device_id=sib, device_id_type=MESH,
        )
        sends.append((copy, None))

    def got(name, j=0):
        here, when = arrivals.pop((name, j))
        on(when, here.wait_recv)

    def local(i, src, dst, when=None):
        copy = pltpu.make_async_copy(src, dst, ls.at[i])
        on(when, copy.start)
        locals_[i] = (copy, when)

    def got_local(i):
        copy, when = locals_.pop(i)
        on(when, copy.wait)

    def drain():
        for i in list(locals_):
            got_local(i)
        for name, j in list(arrivals):
            got(name, j)
        leave()

    def leave():
        for copy, when in sends:
            on(when, copy.wait_send)
        sends.clear()

    barrier = pltpu.get_barrier_semaphore()
    greet = [sib, dev(xlo, 1 - c, y, z, 1 - xhi), dev(xlo, c, y, z, 1 - xhi)]
    greet += [dev_y(j) for j in (1, 2, 3)] + [dev_z(j) for j in range(1, 8)]
    greet += [back_to(j, i) for j in range(4) for i in range(8) if i in NEAR_ROWS + (6,) and (j, i) != (0, 0)]
    for to in greet:
        pl.semaphore_signal(barrier, inc=1, device_id=to, device_id_type=MESH)

    def far(a, t):
        return jnp.logical_not(jnp.logical_and(same, jnp.logical_and(xlo == a, xhi == t)))

    for a in (0, 1):
        for t in (0, 1):

            @pl.when(jnp.logical_not(jnp.logical_and(same, jnp.logical_and(xlo == a, c == t))))
            def _():
                pl.semaphore_signal(barrier, inc=1, device_id=dev(a, t, y, zt, c), device_id_type=MESH)

            @pl.when(far(a, t))
            def _():
                pl.semaphore_signal(barrier, inc=1, device_id=dev(a, xhi, y, zs, t), device_id_type=MESH)

    local(14, kv_in, kv)
    local(15, sqkv_in, sqkv)
    local(16, order_in, order)
    head = y * 4 + z4
    local(13, cot.at[0], cotb)
    local(0, wkv, wkvb)
    for t in (0, 1):
        local(1 + 16 * t, wo.at[pl.ds(pl.multiple_of(head * 64, 64), 64), pl.ds(t * 512, 512)], wob.at[t])

    got_local(14)
    kvw = kv[0].astype(F32)
    for t in (0, 1):
        kvs[t] = jnp.concatenate(
            [kvw[:, t * 1024:t * 1024 + 512], kvw[:, t * 1024 + 512:t * 1024 + 1024]], axis=0
        ).astype(BF)
    pl.semaphore_wait(barrier, len(greet) + 8 - 2 * same.astype(jnp.int32))

    mine = [jnp.logical_and(kept, c == t) for t in (0, 1)]
    other = [jnp.logical_not(m) for m in mine]
    for t in (0, 1):
        go("kvrow", t, kvs.at[t], kvr.at[xhi], dev(xlo, t, y, z, c), kvr.at[t], when=other[t], rj=xhi)
    local(2, kvs.at[c], kvr.at[xhi], when=kept)
    go("swap_q", 0, points.at[0], qgb.at[0], diag, qgb.at[0], when=swapped)
    local(4, points.at[0], qgb.at[0], when=kept)
    got_local(15)
    sw = sqkv[0].astype(F32)
    pad = jnp.zeros((8, 64), F32)
    for h in range(16):
        top = jnp.concatenate([sw[:, h * 64:h * 64 + 64], sw[:, 1024 + h * 64:1024 + h * 64 + 64]], axis=1)
        low = jnp.concatenate([sw[:, 2048 + h * 64:2048 + h * 64 + 64], pad], axis=1)
        sq[h] = jnp.concatenate([top, low], axis=0).astype(BF)
    for j in FAR_Y:
        go("qy", j - 1, sq.at[pl.ds((y + j) % 4 * 4, 4)], r1.at[y], dev_y(j), None, rj=0, together=True)
    all_here("qy", 0, r1.at[pl.ds(0, 3)])
    all_sent("qy", r1.at[pl.ds(0, 3)])
    local(3, sq.at[pl.ds(y * 4, 4)], r1.at[y])
    got_local(16)
    hot = (lax.broadcasted_iota(jnp.int32, (256, 256), 0) == order[0]).astype(F32).astype(BF)
    got_local(13)
    gsend[...] = tn(hot, cotb[...]).astype(BF)

    go("swap_g", 0, gsend, qgb.at[1], diag, qgb.at[1], when=swapped)
    local(5, gsend, qgb.at[1], when=kept)

    got("kvrow", 0)
    got("kvrow", 1)
    got_local(2)
    p0 = kvr[0].astype(F32)
    p1 = kvr[1].astype(F32)
    left = jnp.concatenate([p0[:8], p1[:8]], axis=0)
    right = jnp.concatenate([p0[8:], p1[8:]], axis=0)
    kv16[c, y, z] = jnp.concatenate([left, right[:, :KA - 512]], axis=1).astype(BF)
    kvb[c, y, z] = right[:, KA - 512:].astype(BF)
    for i in FAR_Y:
        go("ky", i - 1, kv16.at[c, y, z], kv16.at[c, y, z], dev_y(i), None, together=True)
    for j in NEAR_Z:
        go("kz", j - 1, kv16.at[c, y, z], kv16.at[c, y, z], dev_z(j), kv16.at[c, y, zb(j)], together=True)
    all_sent("kz", kv16.at[0, 0, pl.ds(0, 7)])

    def on_along_y(j):
        got("kz", j - 1)
        slot = zb(j)
        for i in FAR_Y:
            go("ky", i - 1, kv16.at[c, y, slot], kv16.at[c, y, slot], dev_y(i), None, together=True)

    for i in FAR_Y:
        go("kyb", i - 1, kvb.at[c, y, z], kvb.at[c, y, z], dev_y(i), kvb.at[c, yb(i), z], together=True)
    all_sent("kyb", kvb.at[0, 0, pl.ds(0, 3)])
    for j in NEAR_Z[:4]:
        on_along_y(j)
    for j in (1, 2, 3):
        got("kyb", j - 1)
    for j in FAR_Z:
        go("kzb", j - 1, kvb.at[c, :, z], kvb.at[c, :, z], dev_z(j), None, rj=0, together=True)
    all_here("kzb", 0, kvb.at[c, :, pl.ds(0, 7)])
    all_sent("kzb", kvb.at[c, :, pl.ds(0, 7)])
    for j in NEAR_Z[4:]:
        on_along_y(j)
    got("qy")
    got_local(3)
    for j in FAR_Z:
        go("qz", j - 1, r1.at[:, (z + j) % 4], r2.at[:, z], dev_z(j), None, rj=0, together=True)
    all_here("qz", 0, r2.at[:, pl.ds(0, 7)])
    all_sent("qz", r2.at[:, pl.ds(0, 7)])
    local(6, r1.at[:, z4], r2.at[:, z])

    all_sent("ky", kv16.at[0, pl.ds(0, 3)])
    go("ks", 0, kv16.at[c, y], kv16.at[c, y], sib, None, together=True)

    got_local(0)
    got("swap_q")
    got_local(4)
    qw = nt(qgb[0], wkvb[:, 0:1024]).astype(BF)
    qg[0, 0:256] = qw[:, 0:512]
    qg[1, 0:256] = qw[:, 512:1024]

    got("swap_g")
    got_local(5)
    gw = nt(qgb[1], wkvb[:, 1024:2048]).astype(BF)
    qg[0, 256:512] = gw[:, 0:512]
    qg[1, 256:512] = gw[:, 512:1024]

    got("kzb")
    go("ksb", 0, kvb.at[c], kvb.at[c], sib, kvb.at[1 - c])
    for i in (1, 3, 2):
        slot = yb(i)
        all_here("ky", i - 1, kv16.at[c, slot])
        got("ky", i - 1)
        go("ks", 0, kv16.at[c, slot], kv16.at[c, slot], sib, None, together=True)
    all_here("ks", 0, kv16.at[1 - c])
    all_sent("ks", kv16.at[c])
    got("qz")
    got_local(6)
    for t in (0, 1):
        go("qx", t, r2, r3.at[:, :, xhi], dev(xlo, t, y, z, c), r3.at[:, :, t], when=other[t], rj=xhi)
    local(7, r2, r3.at[:, :, xhi], when=kept)

    def product(t):
        return nt(kv16[t].reshape(512, KA), qgb[t, :, 0:KA]) + nt(kvb[t].reshape(512, KB), qgb[t, :, KA:1024])

    mine_first = product(c)
    got("ksb")
    got("ks")
    then = product(1 - c)
    scale = 1.0 / 1024 ** 0.5
    s = jnp.where(c == 0, mine_first, then) * scale
    e = jnp.exp(s - jnp.max(s, axis=0, keepdims=True))
    p = e / jnp.sum(e, axis=0, keepdims=True)
    dp = jnp.where(c == 0, then, mine_first)
    delta = jnp.sum(p * dp, axis=0, keepdims=True)
    ds = (p * (dp - delta) * scale).astype(BF)
    pboth[...] = jnp.concatenate([ds, p.astype(BF)], axis=1).reshape(4, 128, 512)

    for i in FAR_Y + (0,):
        yi = (y + i) % 4
        psend[yi] = nn(pboth[yi], qg[1 - c]).astype(BF).reshape(8, 16, 512)
        go("pair", i, psend.at[yi], precv.at[yi], sib, precv.at[yi], together=True)
    for i in FAR_Y + (0,):
        yi = (y + i) % 4
        pown[yi] = nn(pboth[yi], qg[c]).reshape(8, 16, 512)
    all_sent("pair", psend)
    for i in FAR_Y:
        got("pair", i)
    for j in FAR_Z + (0,):
        for i in FAR_Y:
            yi = (y + i) % 4
            zj = (z + j) % 8
            ysend[j, i - 1] = (pown[yi, zj] + precv[yi, zj].astype(F32)).astype(BF)
            go("ry", j * 3 + i - 1, ysend.at[j, i - 1], yrecv.at[j, i - 1], dev_y(i), yrecv.at[j, i - 1], together=True)
    all_sent("ry", ysend)

    gps[:, 0:KA] = tn(ds, kv16[0].reshape(512, KA)).astype(BF)
    gps[:, KA:1024] = tn(ds, kvb[0].reshape(512, KB)).astype(BF)
    go("pts", 0, gps, gpts.at[0], diag, gpts.at[0], when=swapped)
    local(8, gps, gpts.at[0], when=kept)
    got("pair", 0)
    for j in FAR_Z + (0,):
        zj = (z + j) % 8
        acc = pown[y, zj] + precv[y, zj].astype(F32)
        for i in FAR_Y:
            got("ry", j * 3 + i - 1)
            acc = acc + yrecv[j, i - 1].astype(F32)
        if j:
            zsend[j - 1] = acc.astype(BF)
            go("rz", j - 1, zsend.at[j - 1], zrecv.at[j - 1], dev_z(j), None, rj=0, together=True)
    all_here("rz", 0, zrecv)
    all_sent("rz", zsend)
    got("rz")
    for j in range(1, 8):
        acc = acc + zrecv[j - 1].astype(F32)
    dz[c, y, z] = acc.astype(BF)

    for j in NEAR_Z:
        go("gz", j - 1, dz.at[c, y, z], dz.at[c, y, z], dev_z(j), dz.at[c, y, zb(j)], together=True)
    all_sent("gz", dz.at[0, 0, pl.ds(0, 7)])
    for i in FAR_Y:
        go("gy", i - 1, dz.at[c, y, z], dz.at[c, y, z], dev_y(i), None, together=True)
    got("qx", 0)
    got("qx", 1)
    got_local(7)
    tiles = r3[...].astype(F32).reshape(64, 16, 128)
    top = tiles[:, :8].reshape(512, 128)
    low = tiles[:, 8:].reshape(512, 128)
    sq_q = top[:, :64].astype(BF)
    sq_k = top[:, 64:].astype(BF)
    sq_v = low[:, :64].astype(BF)
    kt = top[:, 64:].T.astype(BF)
    vt = low[:, :64].T.astype(BF)

    def near_rows(ref):
        return jnp.concatenate([ref[:, (z + i) % 8, c].astype(F32) for i in NEAR_ROWS], axis=0)

    own = near_rows(r3)
    own_q = own[:, :8].reshape(128, 128)[:, :64].astype(BF)
    own_v = own[:, 8:].reshape(128, 128)[:, :64].astype(BF)
    sscale = 1.0 / 64 ** 0.5

    def columns_softmax(scores):
        weights = jnp.exp(scores - jnp.max(scores, axis=0, keepdims=True))
        return weights / jnp.sum(weights, axis=0, keepdims=True)

    def attend(probs):
        high = probs.astype(BF)
        rounded = nn(vt, high)
        return rounded, rounded + nn(vt, (probs - high.astype(F32)).astype(BF))

    sprobs = columns_softmax(nt(sq_k, sq_q) * sscale)
    spt[...] = sprobs.reshape(4, 8, 2, 8, 512)
    attended, ot[...] = attend(sprobs)
    att[...] = attended.astype(BF)
    sprobs = columns_softmax(nt(sq_k, own_q) * sscale)
    spi[...] = sprobs
    _, oti[...] = attend(sprobs)

    for j in NEAR_Z:
        got("gz", j - 1)
        slot = zb(j)
        for i in FAR_Y:
            go("gy", i - 1, dz.at[c, y, slot], dz.at[c, y, slot], dev_y(i), None, together=True)
    all_sent("gy", dz.at[0, pl.ds(0, 3)])
    go("gs", 0, dz.at[c, y], dz.at[c, y], sib, None, together=True)
    for i in (1, 3, 2):
        slot = yb(i)
        all_here("gy", i - 1, dz.at[c, slot])
        got("gy", i - 1)
        go("gs", 0, dz.at[c, slot], dz.at[c, slot], sib, None, together=True)
    all_here("gs", 0, dz.at[1 - c])
    all_sent("gs", dz.at[c])
    got_local(1)
    got_local(17)
    datt = nt(dz[c].reshape(512, 512), wob[c])
    got("gs")

    dz0 = dz[0].reshape(512, 512)
    dz1 = dz[1].reshape(512, 512)
    datt = datt + nt(dz[1 - c].reshape(512, 512), wob[1 - c])
    datt = datt.astype(BF)
    dattw = datt.astype(F32)
    dat[...] = dattw.reshape(4, 8, 2, 8, 64)
    own_datt = near_rows(dat).reshape(128, 64)
    sdelta = jnp.sum(dattw.T * ot[...], axis=0, keepdims=True)
    own_sdelta = jnp.sum(own_datt.T * oti[...], axis=0, keepdims=True)
    rows_p = near_rows(spt).reshape(128, 512)
    sds = (rows_p * (nt(own_v, datt) - sdelta) * sscale).astype(BF)
    dk = nn(sds, sq_q)
    dv = nn(rows_p.astype(BF), datt)
    sds = (spi[...] * (nt(sq_v, own_datt.astype(BF)) - own_sdelta) * sscale).astype(BF)
    dq = nn(kt, sds).T
    m1 = jnp.concatenate([dq, dk], axis=1).reshape(16, 8, 128)
    m2 = jnp.concatenate([dv, jnp.zeros((128, 64), F32)], axis=1).reshape(16, 8, 128)
    ob[...] = jnp.concatenate([m1, m2], axis=1).astype(BF).reshape(4, 4, 16, 128)

    for at, i in reversed(list(enumerate(NEAR_ROWS))):
        for j in (2, 1, 3, 0):
            go("back", j * 4 + at, ob.at[at, (y + j) % 4], or2.at[y, z4], back_to(j, i),
               or2.at[yb(j), (z + 8 - i) % 4], when=None if j + i else swapped)
    local(11, ob.at[0, y], or2.at[y, z4], when=kept)

    pjf[:, 0:512] = nn(att[...], dz0)
    pjf[:, 512:1024] = nn(att[...], dz1)
    pjs[...] = pjf[pl.ds(pl.multiple_of((z // 4 * 2 + c) * 16, 16), 16), :].astype(BF)
    shape_at = xlo * 2 + xhi
    for a in (0, 1):
        for t in (0, 1):
            away = jnp.logical_not(jnp.logical_and(same, jnp.logical_and(xlo == a, c == t)))
            go("proj", a * 2 + t, pjs, pjr.at[shape_at], dev(a, t, y, zt, c), pjr.at[a * 2 + t], when=away, rj=shape_at)
    local(9, pjs, pjr.at[shape_at], when=same)

    rows = [dz[t, y, z].astype(F32) for t in (0, 1)]
    first = c == 0
    gls[...] = jnp.concatenate([jnp.where(first, r[:8], r[8:]) for r in rows], axis=0).astype(BF)
    go("lat", 0, gls, glr, diag, glr, when=swapped)
    local(10, gls, glr, when=kept)
    leave()
    drain()


def finish(pts_in, or2_in, glr_in, pjr_in, gpts_out, glat_out, gqkv_out, gproj_out,
           pts, or2, glr, pjr, glat, gqkv, gproj, sem):
    def copy(i, src, dst):
        moved = pltpu.make_async_copy(src, dst, sem.at[i])
        moved.start()
        return moved

    loads = [copy(0, pts_in, pts), copy(1, pjr_in, pjr), copy(2, glr_in, glr), copy(3, or2_in, or2)]
    loads[0].wait()
    stores = [copy(4, pts, gpts_out)]
    loads[1].wait()
    total = pjr[0].astype(F32)
    for src in (1, 2, 3):
        total = total + pjr[src].astype(F32)
    gproj[...] = total
    stores.append(copy(5, gproj, gproj_out))
    loads[2].wait()
    lr = glr[...].astype(F32)
    glat[0] = jnp.concatenate([lr[:8], lr[8:]], axis=1).astype(BF)
    stores.append(copy(6, glat, glat_out))
    loads[3].wait()
    res = or2[...].astype(F32).reshape(16, 16, 128)
    parts = [res[h, :8, 0:64] for h in range(16)]
    parts += [res[h, :8, 64:128] for h in range(16)]
    parts += [res[h, 8:, 0:64] for h in range(16)]
    gqkv[0] = jnp.concatenate(parts, axis=1).astype(BF)
    stores.append(copy(7, gqkv, gqkv_out))
    for moved in stores:
        moved.wait()


def on_device(points, order, cotangent, kv_cross, self_qkv, kv_weight, out_weight):
    hbm = pl.BlockSpec(memory_space=pl.ANY)
    scratch = [
        ((1, 1, 256), jnp.int32),
        ((1, 8, 2048), BF),
        ((1, 8, 3072), BF),
        ((256, 1024), BF),
        ((256, 1024), BF),
        ((2, 256, 1024), BF),
        ((2, 16, 512), BF),
        ((2, 16, 512), BF),
        ((2, 4, 8, 16, KA), BF),
        ((2, 4, 8, 16, KB), BF),
        ((16, 16, 128), BF),
        ((4, 4, 16, 128), BF),
        ((4, 8, 16, 128), BF),
        ((4, 8, 2, 16, 128), BF),
        ((1024, 2048), BF),
        ((2, 64, 512), BF),
        ((2, 512, 512), BF),
        ((4, 8, 2, 8, 512), F32),
        ((512, 128), F32),
        ((64, 512), BF),
        ((64, 512), F32),
        ((64, 128), F32),
        ((4, 128, 512), BF),
        ((4, 8, 16, 512), BF),
        ((4, 8, 16, 512), BF),
        ((4, 8, 16, 512), F32),
        ((8, 3, 16, 512), BF),
        ((8, 3, 16, 512), BF),
        ((7, 16, 512), BF),
        ((7, 16, 512), BF),
        ((2, 4, 8, 16, 512), BF),
        ((4, 8, 2, 8, 64), F32),
        ((64, 1024), F32),
        ((16, 1024), BF),
        ((4, 4, 16, 128), BF),
        ((16, 512), BF),
        ((256, 1024), BF),
    ]
    parts = pl.pallas_call(
        kernel,
        out_shape=(
            jax.ShapeDtypeStruct((1, 256, 1024), BF),
            jax.ShapeDtypeStruct((4, 4, 16, 128), BF),
            jax.ShapeDtypeStruct((16, 512), BF),
            jax.ShapeDtypeStruct((4, 16, 1024), BF),
        ),
        in_specs=[hbm] * 7,
        out_specs=(hbm, hbm, hbm, hbm),
        scratch_shapes=[pltpu.VMEM(shape, dtype) for shape, dtype in scratch]
        + [pltpu.SemaphoreType.DMA((COUNT,)), pltpu.SemaphoreType.DMA((COUNT,)), pltpu.SemaphoreType.DMA((18,))],
        name="fused_backward",
        cost_estimate=pl.CostEstimate(flops=3_000_000_000, bytes_accessed=8_000_000, transcendentals=400_000),
        compiler_params=pltpu.CompilerParams(
            collective_id=0, has_side_effects=True, vmem_limit_bytes=56 * 1024 * 1024
        ),
    )(points, order, cotangent, kv_cross, self_qkv, kv_weight, out_weight)
    return pl.pallas_call(
        finish,
        out_shape=(
            jax.ShapeDtypeStruct((1, 256, 1024), BF),
            jax.ShapeDtypeStruct((1, 8, 1024), BF),
            jax.ShapeDtypeStruct((1, 8, 3072), BF),
            jax.ShapeDtypeStruct((16, 1024), F32),
        ),
        in_specs=[hbm] * 4,
        out_specs=(hbm,) * 4,
        scratch_shapes=[
            pltpu.VMEM((1, 256, 1024), BF),
            pltpu.VMEM((4, 4, 16, 128), BF),
            pltpu.VMEM((16, 512), BF),
            pltpu.VMEM((4, 16, 1024), BF),
            pltpu.VMEM((1, 8, 1024), BF),
            pltpu.VMEM((1, 8, 3072), BF),
            pltpu.VMEM((16, 1024), F32),
            pltpu.SemaphoreType.DMA((8,)),
        ],
        name="finish",
        cost_estimate=pl.CostEstimate(flops=100_000, bytes_accessed=1_500_000, transcendentals=0),
    )(*parts)


def solution(mesh):
    rows = P("batch", "query", None)
    return jax.shard_map(
        on_device,
        mesh=mesh,
        in_specs=(rows, rows, rows, rows, rows, P(), P()),
        out_specs=(rows, rows, rows, P("query", None)),
        check_vma=False,
    )
```

```python
import functools

import jax
import jax.numpy as jnp
from jax import lax
from jax.experimental import pallas as pl
from jax.experimental.pallas import tpu as pltpu
from jax.sharding import PartitionSpec as P

MESH = pl.DeviceIdType.MESH
BF = jnp.bfloat16
F32 = jnp.float32


def nt(a, b):
    return lax.dot_general(a, b, (((1,), (1,)), ((), ())), preferred_element_type=F32)


def nn(a, b):
    return lax.dot_general(a, b, (((1,), (0,)), ((), ())), preferred_element_type=F32)


def tn(a, b):
    return lax.dot_general(a, b, (((0,), (0,)), ((), ())), preferred_element_type=F32)


GROUPS = dict(
    kvrow=2, qy=3, qz=7, qx=2, swap_q=1, swap_g=1, kz=7, ky=3, ks=1, kyb=3, kzb=7, ksb=1,
    pair=4, ry=24, rz=7, gz=7, gy=24, gs=4, lat=1, proj=4, back=16, pts=1,
)
KA, KB = 896, 128
MIX_Z = (4, 1, 7, 2, 6, 3, 5)
FAR_Z = (4, 3, 5, 2, 6, 1, 7)
NEAR_Z = (1, 7, 2, 6, 3, 5, 4)
ARRIVE_Z = (1, 7, 2, 6, 4, 3, 5)
FAR_Y = (2, 1, 3)
NEAR_ROWS = (0, 1, 7, 2)
BASE = {}
COUNT = 0
for _name, _n in GROUPS.items():
    BASE[_name] = COUNT
    COUNT += _n


def kernel(
    points, order_in, cot, kv_in, sqkv_in, wkv, wo,
    gpts, or2, glr, pjr,
    order, kv, sqkv, cotb, gsend, qgb, kvs, kvr, kv16, kvb, sq, r1, r2, r3, wkvb, wob, qg, spt, spi, att, ot, oti,
    pboth, psend, precv, pown, ysend, yrecv, zsend, zrecv, dz,
    dat, pjf, pjs, ob, gls, gps,
    ss, rs, ls,
):
    b = lax.axis_index("batch")
    k = lax.axis_index("query")
    xlo = b // 2
    c = b % 2
    y = k // 16
    z = (k // 2) % 8
    xhi = k % 2
    swapped = c != xhi
    kept = c == xhi

    def dev(xlo_, c_, y_, z_, xhi_):
        return (xlo_ * 2 + c_, (y_ * 8 + z_) * 2 + xhi_)

    sib = dev(xlo, 1 - c, y, z, xhi)
    diag = dev(xlo, xhi, y, z, c)
    z4 = z % 4
    zt = 2 * z4 + z // 4
    zs = z // 2 + 4 * (z % 2)
    same = jnp.logical_and(kept, z == zt)

    def dev_y(j):
        return dev(xlo, c, (y + j) % 4, z, xhi)

    def dev_z(j):
        return dev(xlo, c, y, (z + j) % 8, xhi)

    def yb(j):
        return (y + 4 - j) % 4

    def zb(j):
        return (z + 8 - j) % 8

    def back_to(j, i):
        return dev(xlo, xhi, (y + j) % 4, (z + i) % 8, c)

    def on(when, fn):
        if when is None:
            fn()
        else:
            pl.when(when)(fn)

    sends, arrivals, locals_ = [], {}, {}

    def go(name, j, src, dst, to, arrive, when=None, rj=None, together=False):
        i = BASE[name] + j
        copy = pltpu.make_async_remote_copy(
            src_ref=src, dst_ref=dst, send_sem=ss.at[BASE[name] if together else i],
            recv_sem=rs.at[i if rj is None else BASE[name] + rj],
            device_id=to, device_id_type=MESH,
        )
        on(when, copy.start)
        if not together:
            sends.append((copy, when))
        if arrive is not None:
            all_here(name, j, arrive, when)

    def all_here(name, j, arrive, when=None):
        i = BASE[name] + j
        here = pltpu.make_async_remote_copy(
            src_ref=arrive, dst_ref=arrive, send_sem=ss.at[i], recv_sem=rs.at[i],
            device_id=sib, device_id_type=MESH,
        )
        arrivals[name, j] = (here, when)

    def all_sent(name, total):
        i = BASE[name]
        copy = pltpu.make_async_remote_copy(
            src_ref=total, dst_ref=total, send_sem=ss.at[i], recv_sem=rs.at[i],
            device_id=sib, device_id_type=MESH,
        )
        sends.append((copy, None))

    def got(name, j=0):
        here, when = arrivals.pop((name, j))
        on(when, here.wait_recv)

    def local(i, src, dst, when=None):
        copy = pltpu.make_async_copy(src, dst, ls.at[i])
        on(when, copy.start)
        locals_[i] = (copy, when)

    def got_local(i):
        copy, when = locals_.pop(i)
        on(when, copy.wait)

    def drain():
        for i in list(locals_):
            got_local(i)
        for name, j in list(arrivals):
            got(name, j)
        leave()

    def leave():
        for copy, when in sends:
            on(when, copy.wait_send)
        sends.clear()

    barrier = pltpu.get_barrier_semaphore()
    greet = [sib, dev(xlo, 1 - c, y, z, 1 - xhi), dev(xlo, c, y, z, 1 - xhi)]
    greet += [dev_y(j) for j in (1, 2, 3)] + [dev_z(j) for j in range(1, 8)]
    greet += [back_to(j, i) for j in range(4) for i in range(8) if i in NEAR_ROWS + (6,) and (j, i) != (0, 0)]
    for to in reversed(greet):
        pl.semaphore_signal(barrier, inc=1, device_id=to, device_id_type=MESH)

    def far(a, t):
        return jnp.logical_not(jnp.logical_and(same, jnp.logical_and(xlo == a, xhi == t)))

    for a in (0, 1):
        for t in (0, 1):

            @pl.when(jnp.logical_not(jnp.logical_and(same, jnp.logical_and(xlo == a, c == t))))
            def _():
                pl.semaphore_signal(barrier, inc=1, device_id=dev(a, t, y, zt, c), device_id_type=MESH)

            @pl.when(far(a, t))
            def _():
                pl.semaphore_signal(barrier, inc=1, device_id=dev(a, xhi, y, zs, t), device_id_type=MESH)

    local(14, kv_in, kv)
    local(15, sqkv_in, sqkv)
    local(16, order_in, order)
    head = y * 4 + z4
    local(13, cot.at[0], cotb)
    local(0, wkv, wkvb)
    for t in (0, 1):
        local(1 + 16 * t, wo.at[pl.ds(pl.multiple_of(head * 64, 64), 64), pl.ds(t * 512, 512)], wob.at[t])

    got_local(14)
    kvw = kv[0].astype(F32)
    for t in (0, 1):
        kvs[t] = jnp.concatenate(
            [kvw[:, t * 1024:t * 1024 + 512], kvw[:, t * 1024 + 512:t * 1024 + 1024]], axis=0
        ).astype(BF)
    pl.semaphore_wait(barrier, len(greet) + 8 - 2 * same.astype(jnp.int32))

    mine = [jnp.logical_and(kept, c == t) for t in (0, 1)]
    other = [jnp.logical_not(m) for m in mine]
    for t in (0, 1):
        go("kvrow", t, kvs.at[t], kvr.at[xhi], dev(xlo, t, y, z, c), kvr.at[t], when=other[t], rj=xhi)
    local(2, kvs.at[c], kvr.at[xhi], when=kept)
    go("swap_q", 0, points.at[0], qgb.at[0], diag, qgb.at[0], when=swapped)
    local(4, points.at[0], qgb.at[0], when=kept)
    got_local(15)
    sw = sqkv[0].astype(F32)
    pad = jnp.zeros((8, 64), F32)
    for h in range(16):
        top = jnp.concatenate([sw[:, h * 64:h * 64 + 64], sw[:, 1024 + h * 64:1024 + h * 64 + 64]], axis=1)
        low = jnp.concatenate([sw[:, 2048 + h * 64:2048 + h * 64 + 64], pad], axis=1)
        sq[h] = jnp.concatenate([top, low], axis=0).astype(BF)
    for j in FAR_Y:
        go("qy", j - 1, sq.at[pl.ds((y + j) % 4 * 4, 4)], r1.at[y], dev_y(j), None, rj=0, together=True)
    all_here("qy", 0, r1.at[pl.ds(0, 3)])
    all_sent("qy", r1.at[pl.ds(0, 3)])
    local(3, sq.at[pl.ds(y * 4, 4)], r1.at[y])
    got_local(16)
    hot = (lax.broadcasted_iota(jnp.int32, (256, 256), 0) == order[0]).astype(F32).astype(BF)
    got_local(13)
    gsend[...] = tn(hot, cotb[...]).astype(BF)

    go("swap_g", 0, gsend, qgb.at[1], diag, qgb.at[1], when=swapped)
    local(5, gsend, qgb.at[1], when=kept)

    got("kvrow", 0)
    got("kvrow", 1)
    got_local(2)
    p0 = kvr[0].astype(F32)
    p1 = kvr[1].astype(F32)
    left = jnp.concatenate([p0[:8], p1[:8]], axis=0)
    right = jnp.concatenate([p0[8:], p1[8:]], axis=0)
    kv16[c, y, z] = jnp.concatenate([left, right[:, :KA - 512]], axis=1).astype(BF)
    kvb[c, y, z] = right[:, KA - 512:].astype(BF)
    for i in FAR_Y:
        go("ky", i - 1, kv16.at[c, y, z], kv16.at[c, y, z], dev_y(i), None, together=True)
    for j in NEAR_Z:
        go("kz", j - 1, kv16.at[c, y, z], kv16.at[c, y, z], dev_z(j), kv16.at[c, y, zb(j)], together=True)
    all_sent("kz", kv16.at[0, 0, pl.ds(0, 7)])

    def on_along_y(j):
        got("kz", j - 1)
        slot = zb(j)
        for i in FAR_Y:
            go("ky", i - 1, kv16.at[c, y, slot], kv16.at[c, y, slot], dev_y(i), None, together=True)

    for i in FAR_Y:
        go("kyb", i - 1, kvb.at[c, y, z], kvb.at[c, y, z], dev_y(i), kvb.at[c, yb(i), z], together=True)
    all_sent("kyb", kvb.at[0, 0, pl.ds(0, 3)])
    for j in NEAR_Z[:4]:
        on_along_y(j)
    for j in (1, 2, 3):
        got("kyb", j - 1)
    for j in FAR_Z:
        go("kzb", j - 1, kvb.at[c, :, z], kvb.at[c, :, z], dev_z(j), None, rj=0, together=True)
    all_here("kzb", 0, kvb.at[c, :, pl.ds(0, 7)])
    all_sent("kzb", kvb.at[c, :, pl.ds(0, 7)])
    for j in NEAR_Z[4:]:
        on_along_y(j)
    got("qy")
    got_local(3)
    for j in FAR_Z:
        go("qz", j - 1, r1.at[:, (z + j) % 4], r2.at[:, z], dev_z(j), None, rj=0, together=True)
    all_here("qz", 0, r2.at[:, pl.ds(0, 7)])
    all_sent("qz", r2.at[:, pl.ds(0, 7)])
    local(6, r1.at[:, z4], r2.at[:, z])

    all_sent("ky", kv16.at[0, pl.ds(0, 3)])
    go("ks", 0, kv16.at[c, y], kv16.at[c, y], sib, None, together=True)

    got_local(0)
    got("swap_q")
    got_local(4)
    qw = nt(qgb[0], wkvb[:, 0:1024]).astype(BF)
    qg[0, 0:256] = qw[:, 0:512]
    qg[1, 0:256] = qw[:, 512:1024]

    got("swap_g")
    got_local(5)
    gw = nt(qgb[1], wkvb[:, 1024:2048]).astype(BF)
    qg[0, 256:512] = gw[:, 0:512]
    qg[1, 256:512] = gw[:, 512:1024]

    got("kzb")
    go("ksb", 0, kvb.at[c], kvb.at[c], sib, kvb.at[1 - c])
    for i in (1, 3, 2):
        slot = yb(i)
        all_here("ky", i - 1, kv16.at[c, slot])
        got("ky", i - 1)
        go("ks", 0, kv16.at[c, slot], kv16.at[c, slot], sib, None, together=True)
    all_here("ks", 0, kv16.at[1 - c])
    all_sent("ks", kv16.at[c])
    got("qz")
    got_local(6)
    for t in (0, 1):
        go("qx", t, r2, r3.at[:, :, xhi], dev(xlo, t, y, z, c), r3.at[:, :, t], when=other[t], rj=xhi)
    local(7, r2, r3.at[:, :, xhi], when=kept)

    def product(t):
        return nt(kv16[t].reshape(512, KA), qgb[t, :, 0:KA]) + nt(kvb[t].reshape(512, KB), qgb[t, :, KA:1024])

    mine_first = product(c)
    got("ksb")
    got("ks")
    then = product(1 - c)
    scale = 1.0 / 1024 ** 0.5
    s = jnp.where(c == 0, mine_first, then) * scale
    e = jnp.exp(s - jnp.max(s, axis=0, keepdims=True))
    p = e / jnp.sum(e, axis=0, keepdims=True)
    dp = jnp.where(c == 0, then, mine_first)
    delta = jnp.sum(p * dp, axis=0, keepdims=True)
    ds = (p * (dp - delta) * scale).astype(BF)
    pboth[...] = jnp.concatenate([ds, p.astype(BF)], axis=1).reshape(4, 128, 512)

    def for_sibling(i):
        yi = (y + i) % 4
        psend[yi] = nn(pboth[yi], qg[1 - c]).astype(BF).reshape(8, 16, 512)
        go("pair", i, psend.at[yi], precv.at[yi], sib, precv.at[yi], together=True)

    def for_own(i):
        yi = (y + i) % 4
        pown[yi] = nn(pboth[yi], qg[c]).reshape(8, 16, 512)

    for i in FAR_Y:
        for_sibling(i)
    for i in FAR_Y:
        for_own(i)
    for i in FAR_Y:
        got("pair", i)
    for j in FAR_Z + (0,):
        for i in FAR_Y:
            yi = (y + i) % 4
            zj = (z + j) % 8
            ysend[j, i - 1] = (pown[yi, zj] + precv[yi, zj].astype(F32)).astype(BF)
            go("ry", j * 3 + i - 1, ysend.at[j, i - 1], yrecv.at[j, i - 1], dev_y(i), yrecv.at[j, i - 1], together=True)
    for_sibling(0)
    for_own(0)
    all_sent("pair", psend)
    all_sent("ry", ysend)

    gps[:, 0:KA] = tn(ds, kv16[0].reshape(512, KA)).astype(BF)
    gps[:, KA:1024] = tn(ds, kvb[0].reshape(512, KB)).astype(BF)
    go("pts", 0, gps, gpts.at[0], diag, gpts.at[0], when=swapped)
    local(8, gps, gpts.at[0], when=kept)
    got("pair", 0)
    for j in FAR_Z + (0,):
        zj = (z + j) % 8
        acc = pown[y, zj] + precv[y, zj].astype(F32)
        for i in FAR_Y:
            got("ry", j * 3 + i - 1)
            acc = acc + yrecv[j, i - 1].astype(F32)
        if j:
            zsend[j - 1] = acc.astype(BF)
            go("rz", j - 1, zsend.at[j - 1], zrecv.at[j - 1], dev_z(j), None, rj=0, together=True)
    all_here("rz", 0, zrecv)
    all_sent("rz", zsend)
    got("rz")
    for j in range(1, 8):
        acc = acc + zrecv[j - 1].astype(F32)
    dz[c, y, z] = acc.astype(BF)

    for j in NEAR_Z:
        go("gz", j - 1, dz.at[c, y, z], dz.at[c, y, z], dev_z(j), dz.at[c, y, zb(j)], together=True)
    all_sent("gz", dz.at[0, 0, pl.ds(0, 7)])
    for i in FAR_Y:
        go("gy", i - 1, dz.at[c, y, z], dz.at[c, y, z], dev_y(i), None, together=True)
    got("qx", 0)
    got("qx", 1)
    got_local(7)
    tiles = r3[...].astype(F32).reshape(64, 16, 128)
    top = tiles[:, :8].reshape(512, 128)
    low = tiles[:, 8:].reshape(512, 128)
    sq_q = top[:, :64].astype(BF)
    sq_k = top[:, 64:].astype(BF)
    sq_v = low[:, :64].astype(BF)
    kt = top[:, 64:].T.astype(BF)
    vt = low[:, :64].T.astype(BF)

    def near_rows(ref):
        return jnp.concatenate([ref[:, (z + i) % 8, c].astype(F32) for i in NEAR_ROWS], axis=0)

    own = near_rows(r3)
    own_q = own[:, :8].reshape(128, 128)[:, :64].astype(BF)
    own_v = own[:, 8:].reshape(128, 128)[:, :64].astype(BF)
    sscale = 1.0 / 64 ** 0.5

    def columns_softmax(scores):
        weights = jnp.exp(scores - jnp.max(scores, axis=0, keepdims=True))
        return weights / jnp.sum(weights, axis=0, keepdims=True)

    def attend(probs):
        high = probs.astype(BF)
        rounded = nn(vt, high)
        return rounded, rounded + nn(vt, (probs - high.astype(F32)).astype(BF))

    sprobs = columns_softmax(nt(sq_k, sq_q) * sscale)
    spt[...] = sprobs.reshape(4, 8, 2, 8, 512)
    attended, ot[...] = attend(sprobs)
    att[...] = attended.astype(BF)
    sprobs = columns_softmax(nt(sq_k, own_q) * sscale)
    spi[...] = sprobs
    _, oti[...] = attend(sprobs)

    for j in NEAR_Z:
        got("gz", j - 1)
        slot = zb(j)
        for i in FAR_Y:
            go("gy", i - 1, dz.at[c, y, slot], dz.at[c, y, slot], dev_y(i), None, together=True)
    all_sent("gy", dz.at[0, pl.ds(0, 3)])
    go("gs", 0, dz.at[c, y], dz.at[c, y], sib, None, together=True)
    for i in (1, 3, 2):
        slot = yb(i)
        all_here("gy", i - 1, dz.at[c, slot])
        got("gy", i - 1)
        go("gs", 0, dz.at[c, slot], dz.at[c, slot], sib, None, together=True)
    all_here("gs", 0, dz.at[1 - c])
    all_sent("gs", dz.at[c])
    got_local(1)
    got_local(17)
    datt = nt(dz[c].reshape(512, 512), wob[c])
    got("gs")

    dz0 = dz[0].reshape(512, 512)
    dz1 = dz[1].reshape(512, 512)
    datt = datt + nt(dz[1 - c].reshape(512, 512), wob[1 - c])
    datt = datt.astype(BF)
    dattw = datt.astype(F32)
    dat[...] = dattw.reshape(4, 8, 2, 8, 64)
    own_datt = near_rows(dat).reshape(128, 64)
    sdelta = jnp.sum(dattw.T * ot[...], axis=0, keepdims=True)
    own_sdelta = jnp.sum(own_datt.T * oti[...], axis=0, keepdims=True)
    rows_p = near_rows(spt).reshape(128, 512)
    sds = (rows_p * (nt(own_v, datt) - sdelta) * sscale).astype(BF)
    dk = nn(sds, sq_q)
    dv = nn(rows_p.astype(BF), datt)
    sds = (spi[...] * (nt(sq_v, own_datt.astype(BF)) - own_sdelta) * sscale).astype(BF)
    dq = nn(kt, sds).T
    m1 = jnp.concatenate([dq, dk], axis=1).reshape(16, 8, 128)
    m2 = jnp.concatenate([dv, jnp.zeros((128, 64), F32)], axis=1).reshape(16, 8, 128)
    ob[...] = jnp.concatenate([m1, m2], axis=1).astype(BF).reshape(4, 4, 16, 128)

    for at, i in reversed(list(enumerate(NEAR_ROWS))):
        for j in (2, 1, 3, 0):
            go("back", j * 4 + at, ob.at[at, (y + j) % 4], or2.at[y, z4], back_to(j, i),
               or2.at[yb(j), (z + 8 - i) % 4], when=None if j + i else swapped)
    local(11, ob.at[0, y], or2.at[y, z4], when=kept)

    pjf[:, 0:512] = nn(att[...], dz0)
    pjf[:, 512:1024] = nn(att[...], dz1)
    pjs[...] = pjf[pl.ds(pl.multiple_of((z // 4 * 2 + c) * 16, 16), 16), :].astype(BF)
    shape_at = xlo * 2 + xhi
    for a in (0, 1):
        for t in (0, 1):
            away = jnp.logical_not(jnp.logical_and(same, jnp.logical_and(xlo == a, c == t)))
            go("proj", a * 2 + t, pjs, pjr.at[shape_at], dev(a, t, y, zt, c), pjr.at[a * 2 + t], when=away, rj=shape_at)
    local(9, pjs, pjr.at[shape_at], when=same)

    rows = [dz[t, y, z].astype(F32) for t in (0, 1)]
    first = c == 0
    gls[...] = jnp.concatenate([jnp.where(first, r[:8], r[8:]) for r in rows], axis=0).astype(BF)
    go("lat", 0, gls, glr, diag, glr, when=swapped)
    local(10, gls, glr, when=kept)
    leave()
    drain()


def finish(pts_in, or2_in, glr_in, pjr_in, gpts_out, glat_out, gqkv_out, gproj_out,
           pts, or2, glr, pjr, glat, gqkv, gproj, sem):
    def copy(i, src, dst):
        moved = pltpu.make_async_copy(src, dst, sem.at[i])
        moved.start()
        return moved

    loads = [copy(0, pts_in, pts), copy(1, pjr_in, pjr), copy(2, glr_in, glr), copy(3, or2_in, or2)]
    loads[0].wait()
    stores = [copy(4, pts, gpts_out)]
    loads[1].wait()
    total = pjr[0].astype(F32)
    for src in (1, 2, 3):
        total = total + pjr[src].astype(F32)
    gproj[...] = total
    stores.append(copy(5, gproj, gproj_out))
    loads[2].wait()
    lr = glr[...].astype(F32)
    glat[0] = jnp.concatenate([lr[:8], lr[8:]], axis=1).astype(BF)
    stores.append(copy(6, glat, glat_out))
    loads[3].wait()
    res = or2[...].astype(F32).reshape(16, 16, 128)
    parts = [res[h, :8, 0:64] for h in range(16)]
    parts += [res[h, :8, 64:128] for h in range(16)]
    parts += [res[h, 8:, 0:64] for h in range(16)]
    gqkv[0] = jnp.concatenate(parts, axis=1).astype(BF)
    stores.append(copy(7, gqkv, gqkv_out))
    for moved in stores:
        moved.wait()


def on_device(points, order, cotangent, kv_cross, self_qkv, kv_weight, out_weight):
    hbm = pl.BlockSpec(memory_space=pl.ANY)
    scratch = [
        ((1, 1, 256), jnp.int32),
        ((1, 8, 2048), BF),
        ((1, 8, 3072), BF),
        ((256, 1024), BF),
        ((256, 1024), BF),
        ((2, 256, 1024), BF),
        ((2, 16, 512), BF),
        ((2, 16, 512), BF),
        ((2, 4, 8, 16, KA), BF),
        ((2, 4, 8, 16, KB), BF),
        ((16, 16, 128), BF),
        ((4, 4, 16, 128), BF),
        ((4, 8, 16, 128), BF),
        ((4, 8, 2, 16, 128), BF),
        ((1024, 2048), BF),
        ((2, 64, 512), BF),
        ((2, 512, 512), BF),
        ((4, 8, 2, 8, 512), F32),
        ((512, 128), F32),
        ((64, 512), BF),
        ((64, 512), F32),
        ((64, 128), F32),
        ((4, 128, 512), BF),
        ((4, 8, 16, 512), BF),
        ((4, 8, 16, 512), BF),
        ((4, 8, 16, 512), F32),
        ((8, 3, 16, 512), BF),
        ((8, 3, 16, 512), BF),
        ((7, 16, 512), BF),
        ((7, 16, 512), BF),
        ((2, 4, 8, 16, 512), BF),
        ((4, 8, 2, 8, 64), F32),
        ((64, 1024), F32),
        ((16, 1024), BF),
        ((4, 4, 16, 128), BF),
        ((16, 512), BF),
        ((256, 1024), BF),
    ]
    parts = pl.pallas_call(
        kernel,
        out_shape=(
            jax.ShapeDtypeStruct((1, 256, 1024), BF),
            jax.ShapeDtypeStruct((4, 4, 16, 128), BF),
            jax.ShapeDtypeStruct((16, 512), BF),
            jax.ShapeDtypeStruct((4, 16, 1024), BF),
        ),
        in_specs=[hbm] * 7,
        out_specs=(hbm, hbm, hbm, hbm),
        scratch_shapes=[pltpu.VMEM(shape, dtype) for shape, dtype in scratch]
        + [pltpu.SemaphoreType.DMA((COUNT,)), pltpu.SemaphoreType.DMA((COUNT,)), pltpu.SemaphoreType.DMA((18,))],
        name="fused_backward",
        cost_estimate=pl.CostEstimate(flops=3_000_000_000, bytes_accessed=8_000_000, transcendentals=400_000),
        compiler_params=pltpu.CompilerParams(
            collective_id=0, has_side_effects=True, vmem_limit_bytes=56 * 1024 * 1024
        ),
    )(points, order, cotangent, kv_cross, self_qkv, kv_weight, out_weight)
    return pl.pallas_call(
        finish,
        out_shape=(
            jax.ShapeDtypeStruct((1, 256, 1024), BF),
            jax.ShapeDtypeStruct((1, 8, 1024), BF),
            jax.ShapeDtypeStruct((1, 8, 3072), BF),
            jax.ShapeDtypeStruct((16, 1024), F32),
        ),
        in_specs=[hbm] * 4,
        out_specs=(hbm,) * 4,
        scratch_shapes=[
            pltpu.VMEM((1, 256, 1024), BF),
            pltpu.VMEM((4, 4, 16, 128), BF),
            pltpu.VMEM((16, 512), BF),
            pltpu.VMEM((4, 16, 1024), BF),
            pltpu.VMEM((1, 8, 1024), BF),
            pltpu.VMEM((1, 8, 3072), BF),
            pltpu.VMEM((16, 1024), F32),
            pltpu.SemaphoreType.DMA((8,)),
        ],
        name="finish",
        cost_estimate=pl.CostEstimate(flops=100_000, bytes_accessed=1_500_000, transcendentals=0),
    )(*parts)


def solution(mesh):
    rows = P("batch", "query", None)
    return jax.shard_map(
        on_device,
        mesh=mesh,
        in_specs=(rows, rows, rows, rows, rows, P(), P()),
        out_specs=(rows, rows, rows, P("query", None)),
        check_vma=False,
    )
```
